32 devices in a mesh: rows: 8 (over z, y), grp: 4 (over x, core).
Axes of the slice: x: 2, y: 2, z: 4, core: 2. Of those that a mesh axis runs over, the one named last changes fastest.
Arguments:
- start: float32 [256, 65536], P('grp', 'rows'), may hold values from -50 to 50
- momenta: float32 [256, 65536], P('grp', 'rows'), may hold values from -6 to 6
- observed: float32 [65536], P('rows'), may hold values from -6 to 6
- precision_obs: float32 [65536], P('rows'), may hold values from 0.5 to 4
- blocks: float32 [512, 4, 128, 128], P('rows'), may hold values from -0.08 to 9
- block_cols: int32 [512, 4], P('rows'), may hold values from 0 to 511, as said below
- block_count: int32 [512], P('rows'), may hold values from 2 to 4, as said below
- step_size: float32 [1], replicated, may hold values from 0.2 to 0.3
- trajectory: float32 [256], P('grp'), may hold values from 0.3 to 1.5
Outputs:
- position: float32 [256, 65536], P('grp', 'rows')
- momentum: float32 [256, 65536], P('grp', 'rows')
- chees: float32 [256], P('grp')
The draws below stay inside these ranges and needn't reach their ends.
Inputs may be any that keep to these rules, and one draw needn't show every extreme that they name: `block_cols`: slot 0 of block row r names r; slots 1 to 3 name distinct block rows r + k modulo 512 with k from 1 to 64, and k = 64 occurs. `block_count`: 4 is reached.
All inputs are finite; a program needn't handle non-finite values.
Results may differ from the reference program's by a relative error of at most 0.0003.
Values sent between devices are 32-bit elements; how exact they have to be, the bound alone decides.
No kernel may reach another device: no remote copies, remote signals or barrier semaphores. Data moves between devices by JAX's collectives and lax.ppermute only.
A program may use at most 192 MiB of HBM per device.

```python
import math
import jax
import jax.numpy as jnp
from jax import lax

BLOCK = 128
SLOTS = 4
BR_DEV = 64
CHAINS = 256
NBLOCKS = 512
CELLS = 65536


def forced_row(key):
    return jax.random.randint(jax.random.fold_in(key, 11), (), 0, NBLOCKS).astype(jnp.int32)


def draw_block_cols(key, part):
    scores = jax.random.randint(jax.random.fold_in(key, 3), (NBLOCKS, BR_DEV), 0, 2 ** 20) * BR_DEV
    scores = scores + jnp.arange(BR_DEV, dtype=jnp.int32)[None, :]
    order = jnp.argsort(scores, axis=1).astype(jnp.int32)
    offsets = order[:, :SLOTS - 1] + 1
    special = jnp.concatenate([jnp.full((1,), BR_DEV, jnp.int32), jnp.arange(1, SLOTS - 1, dtype=jnp.int32)])
    row_ids = jnp.arange(NBLOCKS, dtype=jnp.int32)
    offsets = jnp.where(row_ids[:, None] == forced_row(key), special[None, :], offsets)
    upper_cols = jnp.mod(row_ids[:, None] + offsets, NBLOCKS)
    return jnp.concatenate([row_ids[:, None], upper_cols], axis=1).astype(jnp.int32)


def draw_block_count(key, part):
    counts = jax.random.randint(jax.random.fold_in(key, 5), (NBLOCKS,), 2, SLOTS + 1)
    row_ids = jnp.arange(NBLOCKS, dtype=jnp.int32)
    return jnp.where(row_ids == forced_row(key), SLOTS, counts).astype(jnp.int32)


def draw_blocks(key, part):
    raw_values = jax.random.uniform(jax.random.fold_in(key, 21), (NBLOCKS, SLOTS, BLOCK, BLOCK), jnp.float32, -1.0, 1.0)
    raw_values = 0.08 * raw_values
    symmetric = 0.5 * (raw_values + jnp.swapaxes(raw_values, 2, 3))
    diag_values = jax.random.uniform(jax.random.fold_in(key, 22), (NBLOCKS, SLOTS, BLOCK, BLOCK), jnp.float32, 5.0, 9.0)
    line_a = jnp.arange(BLOCK)[:, None]
    line_b = jnp.arange(BLOCK)[None, :]
    on_diag = (line_a == line_b)[None, None, :, :]
    slot_zero = jnp.where(on_diag, diag_values, symmetric)
    slot_ids = jnp.arange(SLOTS)[None, :, None, None]
    return jnp.where(slot_ids == 0, slot_zero, raw_values).astype(jnp.float32)


def draw_start(key, part):
    center = 1.5 * jax.random.truncated_normal(jax.random.fold_in(key, 31), -4.0, 4.0, (CELLS,), jnp.float32)
    ramp = jnp.exp(jnp.log(3.0) * jnp.arange(CELLS).astype(jnp.float32) / CELLS)
    jitter = jax.random.truncated_normal(jax.random.fold_in(key, 32), -4.0, 4.0, (CHAINS, CELLS), jnp.float32)
    chain_scale = jnp.ones((CHAINS, 1), jnp.float32)
    return (center[None, :] + 0.8 * chain_scale * ramp[None, :] * jitter).astype(jnp.float32)


def shard_levels(key, shape, pieces, least, largest):
    level, own = 1.0, jax.random.fold_in(key, 6)
    for dim, blocks in pieces:
        heights = jnp.exp(jax.random.uniform(jax.random.fold_in(own, dim), (blocks,), jnp.float32, least / len(pieces), largest / len(pieces)))
        level = level * jnp.repeat(heights, shape[dim] // blocks).reshape([-1 if axis == dim else 1 for axis in range(len(shape))])
    return level


def scatter_about(stream_key, dims, spread, limit, pieces=(), kind=jnp.bfloat16):
    result = jax.random.normal(stream_key, dims, jnp.float32) * spread
    if len(pieces) > 0:
        result = shard_levels(stream_key, dims, pieces, -0.22, 0.18) * result
    return jnp.clip(result, min=-limit, max=limit).astype(kind)


def setup_inputs(seed: int = 0) -> dict:
    key_of = jax.random.split(jax.random.key(seed), 10)
    start = draw_start(jax.random.fold_in(key_of[9], 71), 0)
    momenta = scatter_about(key_of[1], (CHAINS, CELLS), 1.0, 6.0, ((0, 4), (1, 8)), jnp.float32)
    observed = scatter_about(key_of[2], (CELLS,), 1.0, 6.0, ((0, 8),), jnp.float32)
    precision_obs = jnp.clip(jnp.exp(math.log(4.0) - 2.0794415 * jax.random.uniform(key_of[3], (CELLS,), jnp.float32) ** shard_levels(key_of[3], (CELLS,), ((0, 8),), -0.2, 0.2)), 0.5, 4.0)
    blocks = draw_blocks(jax.random.fold_in(key_of[9], 71), 0)
    block_cols = draw_block_cols(jax.random.fold_in(key_of[9], 71), 0)
    block_count = draw_block_count(jax.random.fold_in(key_of[9], 71), 0)
    step_size = jnp.clip(jax.random.uniform(key_of[7], (1,), jnp.float32, 0.2, 0.3), 0.2, 0.3)
    trajectory = jnp.clip(0.3 + 1.2 * jax.random.uniform(key_of[8], (CHAINS,), jnp.float32) ** shard_levels(key_of[8], (CHAINS,), ((0, 4),), -0.2, 0.2), 0.3, 1.5)
    return {"start": start, "momenta": momenta, "observed": observed, "precision_obs": precision_obs, "blocks": blocks, "block_cols": block_cols, "block_count": block_count, "step_size": step_size, "trajectory": trajectory}


PRECISE = lax.Precision.HIGHEST


def apply_precision(latent, blocks, block_cols, block_count):
    chain_total = latent.shape[0]
    block_side = blocks.shape[-1]
    nblocks = blocks.shape[0]
    slot_count = blocks.shape[1]
    block_tiles = latent.reshape(chain_total, nblocks, block_side)
    weights = (jnp.arange(slot_count, dtype=jnp.int32)[None, :] < block_count[:, None]).astype(jnp.float32)

    def group_step(spill_sum, group_id):
        first_row = (group_id * BR_DEV).astype(jnp.int32)
        band_blocks = lax.dynamic_slice_in_dim(blocks, first_row, BR_DEV, 0)
        group_cols = lax.dynamic_slice_in_dim(block_cols, first_row, BR_DEV, 0)
        group_weights = lax.dynamic_slice_in_dim(weights, first_row, BR_DEV, 0)
        group_tiles = lax.dynamic_slice_in_dim(block_tiles, first_row, BR_DEV, 1)
        picked = jnp.take(block_tiles, group_cols, axis=1)
        upper_rows = jnp.einsum("crsb,rsab,rs->cra", picked, band_blocks, group_weights, precision=PRECISE)
        transposed = jnp.einsum("cra,rsab,rs->crsb", group_tiles, band_blocks[:, 1:], group_weights[:, 1:], precision=PRECISE)
        spill_sum = spill_sum.at[:, group_cols[:, 1:]].add(transposed)
        return spill_sum, upper_rows

    spill_sum, upper_rows = lax.scan(group_step, jnp.zeros_like(block_tiles), jnp.arange(nblocks // BR_DEV, dtype=jnp.int32))
    upper_rows = jnp.transpose(upper_rows, (1, 0, 2, 3)).reshape(chain_total, nblocks, block_side)
    return (upper_rows + spill_sum).reshape(chain_total, -1)


def reference(start, momenta, observed, precision_obs, blocks, block_cols, block_count, step_size, trajectory):
    def gradient(latent):
        return -apply_precision(latent, blocks, block_cols, block_count) - precision_obs[None, :] * (latent - observed[None, :])

    step_len = step_size[0]
    half = momenta + (step_len / 2) * gradient(start)
    middle = start + step_len * half
    full = half + step_len * gradient(middle)
    position = middle + step_len * full
    momentum = full + (step_len / 2) * gradient(position)
    mean_start = jnp.sum(start, axis=0) / CHAINS
    mean_end = jnp.sum(position, axis=0) / CHAINS
    offset_start = start - mean_start[None, :]
    offset_end = position - mean_end[None, :]
    spread_start = jnp.sum(offset_start * offset_start, axis=1)
    spread_end = jnp.sum(offset_end * offset_end, axis=1)
    inner = jnp.sum(offset_end * momentum, axis=1)
    chees = trajectory * ((spread_end - spread_start) / CELLS) * (inner / CELLS)
    return position, momentum, chees
```

```python
import functools

import jax
import jax.numpy as jnp
from jax import lax
from jax.experimental import pallas as pl
from jax.experimental.pallas import tpu as pltpu
from jax.sharding import PartitionSpec as P

CHUNKS = 2
GROUP = 4
LIST_AT = 8
ROW_AT = 128
SLOT_AT = 384
PLACE_AT = 640
META = 896

NT = (((1,), (1,)), ((), ()))
NN = (((1,), (0,)), ((), ()))


def passed_along(value, steps):
    count = lax.axis_size("rows")
    pairs = [(source, (source + steps) % count) for source in range(count)]
    return lax.ppermute(value, "rows", pairs)


def product(left, right, dims):
    return lax.dot_general(left, right, dims, preferred_element_type=jnp.float32)


def halves(value):
    high = value.astype(jnp.bfloat16)
    low = (value - high.astype(jnp.float32)).astype(jnp.bfloat16)
    return high, low


def plan_kernel(first_ref, cols_ref, count_ref, meta_ref, local_ref, seen, *, bands, slots, nblocks):
    first = first_ref[0]

    def clear(i, _):
        seen[i] = 0
        return 0

    lax.fori_loop(0, bands, clear, 0)

    def by_row(r, edges):
        live = count_ref[r]
        for s in range(slots):
            raw = cols_ref[r * slots + s] - first
            col = jnp.where(raw < 0, raw + nblocks, raw)
            is_live = s < live
            near = jnp.logical_and(is_live, col < bands)
            far = jnp.logical_and(is_live, col >= bands)
            local_ref[r * slots + s] = jnp.where(near, col, bands)
            meta_ref[ROW_AT + edges] = r
            meta_ref[SLOT_AT + edges] = s
            meta_ref[PLACE_AT + edges] = col - bands
            tile = jnp.where(far, col - bands, bands)
            seen[tile] = 1
            edges = edges + far.astype(jnp.int32)
        return edges

    edges = lax.fori_loop(0, bands, by_row, jnp.int32(0))
    meta_ref[0] = edges

    def by_tile(m, tiles):
        meta_ref[LIST_AT + tiles] = m
        used = seen[m]
        seen[m] = tiles
        return tiles + used

    tiles = lax.fori_loop(0, bands, by_tile, jnp.int32(0))
    meta_ref[1] = tiles

    def by_edge(e, _):
        meta_ref[PLACE_AT + e] = seen[meta_ref[PLACE_AT + e]]
        return 0

    lax.fori_loop(0, edges, by_edge, 0)

    for i in range(GROUP):
        meta_ref[ROW_AT + edges + i] = bands
        meta_ref[SLOT_AT + edges + i] = 0
        meta_ref[PLACE_AT + edges + i] = bands


def near_kernel(
    local_ref, coef_ref, x_ref, v_ref, seen_ref, weight_ref, blocks_ref, out_ref, split, total,
    *, bands, slots, side, step_rows, scale_at,
):
    chains = x_ref.shape[0]
    step = pl.program_id(0)

    @pl.when(step == 0)
    def _():
        high, low = halves(x_ref[...])
        split[:chains, : bands * side] = high
        split[chains:, : bands * side] = low
        split[:, bands * side :] = jnp.zeros((2 * chains, side), jnp.bfloat16)
        total[...] = jnp.zeros_like(total)

    def tile_at(index):
        return pl.ds(pl.multiple_of(index * side, side), side)

    def one_row(i, _):
        r = step * step_rows + i
        cols = [local_ref[r * slots + s] for s in range(slots)]
        high, low = halves(blocks_ref[i])
        both = jnp.concatenate(
            [
                jnp.concatenate([high[s] for s in range(slots)], axis=1),
                jnp.concatenate([low[s] for s in range(slots)], axis=1),
            ],
            axis=0,
        )
        picked = jnp.concatenate([split[:, tile_at(c)] for c in cols], axis=1)
        up = product(picked, both, NT)
        own = split[:, tile_at(r)]
        left = jnp.concatenate(
            [own, jnp.concatenate([own[:chains], jnp.zeros_like(own[:chains])], axis=0)], axis=1
        )
        down = product(left, both[:, side:], NN)
        down = down[:chains] + down[chains:]
        total[:, tile_at(r)] += up[:chains, :side] + (up[:chains, side:] + up[chains:, :side])
        for s in range(1, slots):
            total[:, tile_at(cols[s])] += down[:, (s - 1) * side : s * side]
        return 0

    lax.fori_loop(0, step_rows, one_row, 0, unroll=2)

    @pl.when(step == pl.num_programs(0) - 1)
    def _():
        scale = coef_ref[scale_at]
        pull = total[:, : bands * side] + weight_ref[...] * (x_ref[...] - seen_ref[...])
        out_ref[...] = v_ref[...] - scale * pull


def far_kernel(
    *refs, bands, side, cap, scale_at, receives, sends, step_at=2,
):
    refs = list(refs)
    meta_ref, given_ref, coef_ref = refs[:3]
    refs = refs[3:]
    x_ref, blocks_ref = refs[:2]
    refs = refs[2:]
    if receives:
        w_ref, halo_ref, carry_ref = refs[:3]
        refs = refs[3:]
        new_v = refs.pop(0)
        if sends:
            new_x = refs.pop(0)
    if sends:
        out_halo, out_carry = refs[:2]
        refs = refs[2:]
    raw, both, sems = refs[:3]
    refs = refs[3:]
    if receives:
        vel, halo_split = refs[:2]
        refs = refs[2:]
    if sends:
        split, sum_carry = refs[:2]
    chains = x_ref.shape[0]
    edges = meta_ref[0]
    given = given_ref[1]
    groups = lax.div(edges + GROUP - 1, GROUP)

    def tile_at(index):
        return pl.ds(pl.multiple_of(index * side, side), side)

    def fetch(e):
        return pltpu.make_async_copy(
            blocks_ref.at[meta_ref[ROW_AT + e], meta_ref[SLOT_AT + e]], raw.at[e], sems.at[e]
        )

    def start_fetch(e, _):
        fetch(e).start()
        return 0

    lax.fori_loop(0, edges, start_fetch, 0)

    def ready(e):
        @pl.when(e < edges)
        def _():
            fetch(e).wait()

    def unpack(e):
        high, low = halves(raw[e])
        value = jnp.concatenate([high, low], axis=0)
        return value

    if receives:
        scale = coef_ref[scale_at]
        high, low = halves(halo_ref[...])
        halo_split[:cap, :chains] = high
        halo_split[:cap, chains:] = low
        vel[:, : bands * side] = w_ref[...]

        def add_carry(k, _):
            vel[:, tile_at(given_ref[LIST_AT + k])] -= scale * carry_ref[k]
            return 0

        lax.fori_loop(0, given, add_carry, 0)

        def up_group(g, _):
            sums, rows = [], []
            for i in range(GROUP):
                ready(g * GROUP + i)
            for i in range(GROUP):
                e = g * GROUP + i
                rows.append(meta_ref[ROW_AT + e])
                value = unpack(e)
                if sends:
                    both[e] = value
                place = jnp.minimum(meta_ref[PLACE_AT + e], cap)
                up = product(halo_split[place], value, NT)
                sums.append(up[:chains, :side] + (up[:chains, side:] + up[chains:, :side]))
            for i in range(GROUP):
                vel[:, tile_at(rows[i])] -= scale * sums[i]
            return 0

        lax.fori_loop(0, groups, up_group, 0)
        new_v[...] = vel[:, : bands * side]
        if sends:
            x = x_ref[...] + coef_ref[step_at] * vel[:, : bands * side]
            new_x[...] = x
    else:
        x = x_ref[...]

    if sends:
        high, low = halves(x)
        split[:chains, : bands * side] = high
        split[chains:, : bands * side] = low
        source = new_x if receives else x_ref

        def pack(k, _):
            out_halo[k] = source[:, tile_at(given_ref[LIST_AT + k])]
            return 0

        lax.fori_loop(0, given, pack, 0)
        sum_carry[...] = jnp.zeros_like(sum_carry)

        def down_group(g, _):
            sums, places = [], []
            if not receives:
                for i in range(GROUP):
                    ready(g * GROUP + i)
            for i in range(GROUP):
                e = g * GROUP + i
                row = jnp.minimum(meta_ref[ROW_AT + e], bands)
                places.append(jnp.minimum(meta_ref[PLACE_AT + e], cap))
                value = both[e] if receives else unpack(e)
                own = split[:, tile_at(row)]
                left = jnp.concatenate(
                    [own, jnp.concatenate([own[:chains], jnp.zeros_like(own[:chains])], axis=0)],
                    axis=1,
                )
                down = product(left, value, NN)
                sums.append(down[:chains] + down[chains:])
            for i in range(GROUP):
                sum_carry[places[i]] += sums[i]
            return 0

        lax.fori_loop(0, groups, down_group, 0)
        out_carry[...] = sum_carry[:cap]


SMEM = pl.BlockSpec(memory_space=pltpu.SMEM)
ANY = pl.BlockSpec(memory_space=pl.ANY)


def near_call(local, coef, x, v, seen, weight, blocks, x_at, v_at, scale_at):
    bands, slots, side, _ = blocks.shape
    cells = bands * side
    chains = x_at[1]
    step_rows = 8
    return pl.pallas_call(
        functools.partial(
            near_kernel, bands=bands, slots=slots, side=side, step_rows=step_rows, scale_at=scale_at
        ),
        out_shape=jax.ShapeDtypeStruct((chains, cells), jnp.float32),
        grid=(bands // step_rows,),
        in_specs=[
            SMEM,
            SMEM,
            pl.BlockSpec((chains, cells), lambda i, at=x_at[0]: (at, 0)),
            pl.BlockSpec((chains, cells), lambda i, at=v_at[0]: (at, 0)),
            pl.BlockSpec((1, cells), lambda i: (0, 0)),
            pl.BlockSpec((1, cells), lambda i: (0, 0)),
            pl.BlockSpec((step_rows, slots, side, side), lambda i: (i, 0, 0, 0)),
        ],
        out_specs=pl.BlockSpec((chains, cells), lambda i: (0, 0)),
        scratch_shapes=[
            pltpu.VMEM((2 * chains, cells + side), jnp.bfloat16),
            pltpu.VMEM((chains, cells + side), jnp.float32),
        ],
        compiler_params=pltpu.CompilerParams(vmem_limit_bytes=40 * 2**20),
        cost_estimate=pl.CostEstimate(
            flops=2 * 6 * bands * slots * side * side * chains,
            bytes_accessed=blocks.size * 4 + 4 * chains * cells * 4,
            transcendentals=0,
        ),
        name="near",
    )(local, coef, x, v, seen, weight, blocks)


def far_call(meta, given, coef, x, blocks, w, halo, carry, x_at, scale_at, cap, receives, sends):
    bands, slots, side, _ = blocks.shape
    cells = bands * side
    chains = x_at[1]
    most = bands * (slots - 1) + 8
    whole = pl.BlockSpec((chains, cells), lambda i: (0, 0))
    packed = pl.BlockSpec((cap, chains, side), lambda i: (0, 0, 0))
    state = jax.ShapeDtypeStruct((chains, cells), jnp.float32)
    parcel = jax.ShapeDtypeStruct((cap, chains, side), jnp.float32)
    in_specs = [SMEM, SMEM, SMEM, pl.BlockSpec((chains, cells), lambda i: (x_at[0], 0)), ANY]
    args = [meta, given, coef, x, blocks]
    out_shape, out_specs = [], []
    scratch = [
        pltpu.VMEM((most, side, side), jnp.float32),
        pltpu.VMEM((most, 2 * side, side), jnp.bfloat16),
        pltpu.SemaphoreType.DMA((most,)),
    ]
    if receives:
        in_specs += [whole, packed, packed]
        args += [w, halo, carry]
        out_shape += [state]
        out_specs += [whole]
        scratch += [
            pltpu.VMEM((chains, cells + side), jnp.float32),
            pltpu.VMEM((cap + 1, 2 * chains, side), jnp.bfloat16),
        ]
        if sends:
            out_shape += [state]
            out_specs += [whole]
    if sends:
        out_shape += [parcel, parcel]
        out_specs += [packed, packed]
        scratch += [
            pltpu.VMEM((2 * chains, cells + side), jnp.bfloat16),
            pltpu.VMEM((cap + 1, chains, side), jnp.float32),
        ]
    return pl.pallas_call(
        functools.partial(
            far_kernel, bands=bands, side=side, cap=cap, scale_at=scale_at,
            receives=receives, sends=sends,
        ),
        out_shape=out_shape,
        grid=(1,),
        in_specs=in_specs,
        out_specs=out_specs,
        scratch_shapes=scratch,
        compiler_params=pltpu.CompilerParams(vmem_limit_bytes=52 * 2**20),
        cost_estimate=pl.CostEstimate(
            flops=2 * 6 * bands * side * side * chains,
            bytes_accessed=blocks.size + 4 * chains * cells * 4,
            transcendentals=0,
        ),
        name="far",
    )(*args)


def on_device(
    start, momenta, observed, precision_obs, blocks, block_cols, block_count, step_size, trajectory
):
    bands, slots, side, _ = blocks.shape
    cells = bands * side
    local_chains = start.shape[0]
    chains = local_chains // CHUNKS
    nblocks = bands * lax.axis_size("rows")
    all_cells = cells * lax.axis_size("rows")
    chain_total = local_chains * lax.axis_size("grp")
    first = (lax.axis_index("rows") * bands).astype(jnp.int32).reshape(1)
    meta, local = pl.pallas_call(
        functools.partial(plan_kernel, bands=bands, slots=slots, nblocks=nblocks),
        out_shape=[
            jax.ShapeDtypeStruct((META,), jnp.int32),
            jax.ShapeDtypeStruct((bands * slots,), jnp.int32),
        ],
        in_specs=[SMEM, SMEM, SMEM],
        out_specs=[SMEM, SMEM],
        scratch_shapes=[pltpu.SMEM((bands + 8,), jnp.int32)],
        name="plan",
    )(first, block_cols.reshape(-1), block_count)
    given = passed_along(meta[:ROW_AT], 1)
    step_len = step_size[0]
    coef = jnp.stack([step_len / 2, step_len, step_len])
    seen = observed.reshape(1, cells)
    weight = precision_obs.reshape(1, cells)

    cap = CAP if CAP else bands
    parts = range(CHUNKS)
    far = functools.partial(far_call, meta, given, coef)
    near = functools.partial(near_call, local, coef)
    sent = [
        far(start, blocks, None, None, None, (h, chains), 0, cap, False, True) for h in parts
    ]
    flight = [(passed_along(sent[h][0], -1), passed_along(sent[h][1], 1)) for h in parts]
    x = [start] * CHUNKS
    v = [momenta] * CHUNKS
    at = [(h, chains) for h in parts]
    for turn in range(3):
        scale_at = (0, 1, 0)[turn]
        last = turn == 2
        for h in parts:
            w = near(x[h], v[h], seen, weight, blocks, at[h], at[h], scale_at)
            halo, carry = flight[h]
            result = far(x[h], blocks, w, halo, carry, at[h], scale_at, cap, True, not last)
            if last:
                v[h] = result[0]
            else:
                v[h], x[h] = result[:2]
                flight[h] = (passed_along(result[2], -1), passed_along(result[3], 1))
                at[h] = (0, chains)
    position = jnp.concatenate(x, axis=0)
    momentum = jnp.concatenate(v, axis=0)

    total_start, total_end = lax.psum((jnp.sum(start, axis=0), jnp.sum(position, axis=0)), "grp")
    offset_start = start - (total_start / chain_total)[None, :]
    offset_end = position - (total_end / chain_total)[None, :]
    spread_start, spread_end, inner = lax.psum(
        (
            jnp.sum(offset_start * offset_start, axis=1),
            jnp.sum(offset_end * offset_end, axis=1),
            jnp.sum(offset_end * momentum, axis=1),
        ),
        "rows",
    )
    chees = trajectory * ((spread_end - spread_start) / all_cells) * (inner / all_cells)
    return (position, momentum, chees)


CAP = 0


def solution(mesh):
    placed = (
        P("grp", "rows"),
        P("grp", "rows"),
        P("rows"),
        P("rows"),
        P("rows", None, None, None),
        P("rows", None),
        P("rows"),
        P(),
        P("grp"),
    )
    return jax.shard_map(
        on_device,
        mesh=mesh,
        in_specs=placed,
        out_specs=(P("grp", "rows"), P("grp", "rows"), P("grp")),
        check_vma=False,
    )
```

```python
import functools

import jax
import jax.numpy as jnp
from jax import lax
from jax.experimental import pallas as pl
from jax.experimental.pallas import tpu as pltpu
from jax.sharding import PartitionSpec as P

CHUNKS = 2
GROUP = 12
CAP = 46
VMEM_LIMIT = 60 * 2**20
LIST_AT = 8
ROW_AT = 128
SLOT_AT = 384
PLACE_AT = 640
META = 896

NT = (((1,), (1,)), ((), ()))
NN = (((1,), (0,)), ((), ()))


def passed_along(value, steps):
    count = lax.axis_size("rows")
    pairs = [(source, (source + steps) % count) for source in range(count)]
    return lax.ppermute(value, "rows", pairs)


def product(left, right, dims):
    return lax.dot_general(left, right, dims, preferred_element_type=jnp.float32)


def halves(value):
    high = value.astype(jnp.bfloat16)
    low = (value - high.astype(jnp.float32)).astype(jnp.bfloat16)
    return high, low


def doubled(own, chains):
    top = jnp.concatenate([own[:chains], jnp.zeros_like(own[:chains])], axis=0)
    return jnp.concatenate([own, top], axis=1)


def folded_up(value, chains, side):
    return value[:chains, :side] + (value[:chains, side:] + value[chains:, :side])


def stacked(block):
    high, low = halves(block)
    return jnp.concatenate([high, low], axis=0)


def plan_kernel(first_ref, cols_ref, count_ref, far_ref, near_ref, seen, *, bands, slots, nblocks):
    first = first_ref[0]

    def clear(i, _):
        seen[i] = 0
        return 0

    lax.fori_loop(0, bands, clear, 0, unroll=8)

    def by_row(r, counts):
        edges, nears = counts
        live = count_ref[r]
        for s in range(1, slots):
            raw = cols_ref[s, r] - first
            col = jnp.where(raw < 0, raw + nblocks, raw)
            is_live = s < live
            near = jnp.logical_and(is_live, col < bands)
            far = jnp.logical_and(is_live, col >= bands)
            far_ref[ROW_AT + edges] = r
            far_ref[SLOT_AT + edges] = s
            far_ref[PLACE_AT + edges] = col - bands
            near_ref[ROW_AT + nears] = r
            near_ref[SLOT_AT + nears] = s
            near_ref[PLACE_AT + nears] = col
            seen[jnp.where(far, col - bands, bands)] = 1
            edges = edges + far.astype(jnp.int32)
            nears = nears + near.astype(jnp.int32)
        return edges, nears

    edges, nears = lax.fori_loop(0, bands, by_row, (jnp.int32(0), jnp.int32(0)), unroll=2)
    far_ref[0] = edges
    near_ref[0] = nears

    def by_tile(m, tiles):
        far_ref[LIST_AT + tiles] = m
        used = seen[m]
        seen[m] = tiles
        return tiles + used

    tiles = lax.fori_loop(0, bands, by_tile, jnp.int32(0), unroll=4)
    far_ref[1] = tiles

    def by_edge(e, _):
        far_ref[PLACE_AT + e] = seen[far_ref[PLACE_AT + e]]
        return 0

    lax.fori_loop(0, edges, by_edge, 0)

    for i in range(GROUP):
        far_ref[ROW_AT + edges + i] = bands
        far_ref[SLOT_AT + edges + i] = 0
        far_ref[PLACE_AT + edges + i] = bands
        near_ref[ROW_AT + nears + i] = bands
        near_ref[SLOT_AT + nears + i] = 0
        near_ref[PLACE_AT + nears + i] = bands


def near_kernel(
    list_ref, coef_ref, x_hbm, v_hbm, seen_ref, weight_ref, blocks_hbm, out_hbm,
    x_buf, v_buf, diag, raw, split, total, sems, diag_sems, sem_of,
    *, bands, side, x_row, v_row, scale_at,
):
    chains = x_buf.shape[0]
    cells = bands * side
    edges = list_ref[0]
    groups = lax.div(edges + GROUP - 1, GROUP)
    pieces = diag_sems.shape[0]
    piece = bands // pieces

    def tile_at(index):
        return pl.ds(pl.multiple_of(index * side, side), side)

    get_x = pltpu.make_async_copy(x_hbm.at[pl.ds(x_row, chains)], x_buf, sems.at[0])
    get_v = pltpu.make_async_copy(v_hbm.at[pl.ds(v_row, chains)], v_buf, sems.at[1])
    put_w = pltpu.make_async_copy(v_buf, out_hbm, sems.at[2])

    def fetch_diag(p):
        rows = pl.ds(p * piece, piece)
        return pltpu.make_async_copy(blocks_hbm.at[rows, 0], diag.at[rows], diag_sems.at[p])

    def fetch(e):
        return pltpu.make_async_copy(
            blocks_hbm.at[list_ref[ROW_AT + e], list_ref[SLOT_AT + e]], raw.at[e], sem_of.at[e]
        )

    get_x.start()
    for p in range(pieces):
        fetch_diag(p).start()

    def start_fetch(e, _):
        fetch(e).start()
        return 0

    lax.fori_loop(0, edges, start_fetch, 0)
    get_v.start()
    get_x.wait()
    high, low = halves(x_buf[...])
    split[:chains, :cells] = high
    split[chains:, :cells] = low
    split[:, cells:] = jnp.zeros((2 * chains, side), jnp.bfloat16)
    total[:, cells:] = jnp.zeros((chains, side), jnp.float32)

    def diag_piece(p, _):
        fetch_diag(p).wait()
        for i in range(piece):
            r = p * piece + i
            up = product(split[:, tile_at(r)], stacked(diag[r]), NT)
            total[:, tile_at(r)] = folded_up(up, chains, side)
        return 0

    lax.fori_loop(0, pieces, diag_piece, 0)

    def group(g, _):
        base = g * GROUP
        for i in range(GROUP):

            @pl.when(base + i < edges)
            def _():
                fetch(base + i).wait()

        ups, downs, rows, cols = [], [], [], []
        for i in range(GROUP):
            rows.append(list_ref[ROW_AT + base + i])
            cols.append(list_ref[PLACE_AT + base + i])
            value = stacked(raw[base + i])
            ups.append(folded_up(product(split[:, tile_at(cols[i])], value, NT), chains, side))
            down = product(doubled(split[:, tile_at(rows[i])], chains), value, NN)
            downs.append(down[:chains] + down[chains:])
        for i in range(GROUP):
            total[:, tile_at(rows[i])] += ups[i]
            total[:, tile_at(cols[i])] += downs[i]
        return 0

    lax.fori_loop(0, groups, group, 0)
    get_v.wait()
    pull = total[:, :cells] + weight_ref[...] * (x_buf[...] - seen_ref[...])
    v_buf[...] = v_buf[...] - coef_ref[scale_at] * pull
    put_w.start()
    put_w.wait()


def far_kernel(*refs, bands, side, cap, x_row, scale_at, receives, sends, ends, step_at=2):
    refs = list(refs)

    def take(count):
        taken = refs[:count]
        del refs[:count]
        return taken

    (meta_ref, blocks_hbm) = take(2)
    if receives:
        coef_ref, w_hbm, halo_hbm = take(3)
    if receives and sends:
        given_ref, carry_hbm = take(2)
    if sends:
        (x_hbm,) = take(1)
    if receives:
        (v_out,) = take(1)
    if receives and sends:
        x_out, halo_out = take(2)
    if ends:
        (column_out,) = take(1)
    if sends:
        (carry_out,) = take(1)
    raw, both, sem_of, sems = take(4)
    if receives:
        vel, halo_buf, halo_split = take(3)
    if receives and sends:
        carry_buf, packed_buf = take(2)
    if sends:
        x_buf, split, sum_carry = take(3)
    chains = (vel if receives else x_buf).shape[0]
    cells = bands * side
    edges = meta_ref[0]
    groups = lax.div(edges + GROUP - 1, GROUP)

    def tile_at(index):
        return pl.ds(pl.multiple_of(index * side, side), side)

    def fetch(e):
        return pltpu.make_async_copy(
            blocks_hbm.at[meta_ref[ROW_AT + e], meta_ref[SLOT_AT + e]], raw.at[e], sem_of.at[e]
        )

    def start_fetch(e, _):
        fetch(e).start()
        return 0

    def await_group(base):
        for i in range(GROUP):

            @pl.when(base + i < edges)
            def _():
                fetch(base + i).wait()

    if sends:
        get_x = pltpu.make_async_copy(x_hbm.at[pl.ds(x_row, chains)], x_buf, sems.at[0])
    if receives:
        get_halo = pltpu.make_async_copy(halo_hbm, halo_buf, sems.at[1])
        get_w = pltpu.make_async_copy(w_hbm, vel.at[:, pl.ds(0, cells)], sems.at[2])
        put_v = pltpu.make_async_copy(vel.at[:, pl.ds(0, cells)], v_out, sems.at[3])
        get_halo.start()
        get_w.start()
    if sends and not receives:
        get_x.start()
    lax.fori_loop(0, edges, start_fetch, 0)
    if receives and sends:
        get_carry = pltpu.make_async_copy(carry_hbm, carry_buf, sems.at[4])
        get_carry.start()
        get_x.start()

    if receives:
        scale = coef_ref[scale_at]
        get_halo.wait()
        high, low = halves(halo_buf[...])
        halo_split[:cap, :chains] = high
        halo_split[:cap, chains:] = low
        halo_split[cap] = jnp.zeros((2 * chains, side), jnp.bfloat16)
        get_w.wait()
        vel[:, cells:] = jnp.zeros((chains, side), jnp.float32)

        def up_group(g, _):
            base = g * GROUP
            await_group(base)
            sums, rows = [], []
            for i in range(GROUP):
                rows.append(meta_ref[ROW_AT + base + i])
                value = stacked(raw[base + i])
                if sends:
                    both[base + i] = value
                place = jnp.minimum(meta_ref[PLACE_AT + base + i], cap)
                sums.append(folded_up(product(halo_split[place], value, NT), chains, side))
            for i in range(GROUP):
                vel[:, tile_at(rows[i])] -= scale * sums[i]
            return 0

        lax.fori_loop(0, groups, up_group, 0)
    if receives and sends:
        given = jnp.minimum(given_ref[1], cap)
        get_carry.wait()

        def add_carry(k, _):
            vel[:, tile_at(given_ref[LIST_AT + k])] -= scale * carry_buf[k]
            return 0

        lax.fori_loop(0, given, add_carry, 0)
    if receives:
        put_v.start()
    if sends:
        get_x.wait()
    if receives and sends:
        x_buf[...] += coef_ref[step_at] * vel[:, :cells]
        put_x = pltpu.make_async_copy(x_buf, x_out, sems.at[5])
        put_x.start()
        if ends:
            column_out[...] = jnp.sum(x_buf[...], axis=0, keepdims=True)

        def pack(k, _):
            packed_buf[k] = x_buf[:, tile_at(given_ref[LIST_AT + k])]
            return 0

        lax.fori_loop(0, given, pack, 0)
        put_halo = pltpu.make_async_copy(packed_buf, halo_out, sems.at[6])
        put_halo.start()
    if sends:
        high, low = halves(x_buf[...])
        split[:chains, :cells] = high
        split[chains:, :cells] = low
        split[:, cells:] = jnp.zeros((2 * chains, side), jnp.bfloat16)
        sum_carry[...] = jnp.zeros_like(sum_carry)

        def down_group(g, _):
            base = g * GROUP
            if not receives:
                await_group(base)
            sums, places = [], []
            for i in range(GROUP):
                row = meta_ref[ROW_AT + base + i]
                places.append(jnp.minimum(meta_ref[PLACE_AT + base + i], cap))
                value = both[base + i] if receives else stacked(raw[base + i])
                down = product(doubled(split[:, tile_at(row)], chains), value, NN)
                sums.append(down[:chains] + down[chains:])
            for i in range(GROUP):
                sum_carry[places[i]] += sums[i]
            return 0

        lax.fori_loop(0, groups, down_group, 0)
        put_carry = pltpu.make_async_copy(sum_carry.at[pl.ds(0, cap)], carry_out, sems.at[7])
        put_carry.start()
        put_carry.wait()
    if receives and sends:
        put_x.wait()
        put_halo.wait()
    if receives:
        put_v.wait()


def pack_kernel(given_ref, x_ref, out_ref, *, cap):
    side = out_ref.shape[2]

    def pack(k, _):
        tile = pl.ds(pl.multiple_of(given_ref[LIST_AT + k] * side, side), side)
        out_ref[k] = x_ref[:, tile]
        return 0

    lax.fori_loop(0, jnp.minimum(given_ref[1], cap), pack, 0)


def end_kernel(given_ref, coef_ref, v_ref, carry_ref, off_ref, *rest, cap, scale_at):
    out_ref, dot_ref, sums = rest[-3:]
    side = carry_ref.shape[2]
    scale = coef_ref[scale_at]
    out_ref[...] = v_ref[...]

    def add_carry(k, _):
        tile = pl.ds(pl.multiple_of(given_ref[LIST_AT + k] * side, side), side)
        out_ref[:, tile] -= scale * carry_ref[k]
        return 0

    lax.fori_loop(0, jnp.minimum(given_ref[1], cap), add_carry, 0)
    cells = v_ref.shape[1]
    sums[...] = jnp.zeros_like(sums)
    wide = 8 * side

    def dot(i, _):
        part = pl.ds(pl.multiple_of(i * wide, wide), wide)
        sums[...] += out_ref[:, part] * off_ref[:, part]
        return 0

    lax.fori_loop(0, cells // wide, dot, 0)
    dot_ref[...] = sum(sums[:, i * side : (i + 1) * side] for i in range(8))


def spread_kernel(
    start_ref, *refs, side, chain_total
):
    *x_refs, sum_start_ref, sum_end_ref, position_ref, offset_ref, gain_ref, sums = refs
    chains = x_refs[0].shape[0]
    cells = start_ref.shape[1]
    sums[...] = jnp.zeros_like(sums)
    wide = 4 * side

    def one(i, _):
        part = pl.ds(pl.multiple_of(i * wide, wide), wide)
        mean_start = sum_start_ref[:, part] / chain_total
        mean_end = sum_end_ref[:, part] / chain_total
        for h, x_ref in enumerate(x_refs):
            rows = pl.ds(h * chains, chains)
            x = x_ref[:, part]
            position_ref[rows, part] = x
            off_end = x - mean_end
            offset_ref[rows, part] = off_end
            off_start = start_ref[rows, part] - mean_start
            sums[rows] += off_end * off_end - off_start * off_start
        return 0

    lax.fori_loop(0, cells // wide, one, 0)
    gain_ref[...] = sum(sums[:, i * side : (i + 1) * side] for i in range(4))


SMEM = pl.BlockSpec(memory_space=pltpu.SMEM)
VMEM = pl.BlockSpec(memory_space=pltpu.VMEM)
ANY = pl.BlockSpec(memory_space=pl.ANY)
PARAMS = pltpu.CompilerParams(vmem_limit_bytes=VMEM_LIMIT)
COST = pl.CostEstimate(flops=1000, bytes_accessed=1000, transcendentals=0)


def near_call(near_list, coef, x, v, seen, weight, blocks, chains, x_row, v_row, scale_at):
    bands, slots, side, _ = blocks.shape
    cells = bands * side
    most = bands * (slots - 1) + GROUP
    pieces = 8 if bands % 8 == 0 else 1
    return pl.pallas_call(
        functools.partial(
            near_kernel, bands=bands, side=side, x_row=x_row, v_row=v_row, scale_at=scale_at
        ),
        out_shape=jax.ShapeDtypeStruct((chains, cells), jnp.float32),
        in_specs=[SMEM, SMEM, ANY, ANY, VMEM, VMEM, ANY],
        out_specs=ANY,
        scratch_shapes=[
            pltpu.VMEM((chains, cells), jnp.float32),
            pltpu.VMEM((chains, cells), jnp.float32),
            pltpu.VMEM((bands, side, side), jnp.float32),
            pltpu.VMEM((most, side, side), jnp.float32),
            pltpu.VMEM((2 * chains, cells + side), jnp.bfloat16),
            pltpu.VMEM((chains, cells + side), jnp.float32),
            pltpu.SemaphoreType.DMA((3,)),
            pltpu.SemaphoreType.DMA((pieces,)),
            pltpu.SemaphoreType.DMA((most,)),
        ],
        compiler_params=PARAMS,
        cost_estimate=COST,
        name="near",
    )(near_list, coef, x, v, seen, weight, blocks)


def far_call(meta, given, coef, blocks, x, w, halo, carry, chains, x_row, scale_at, cap, ends=False):
    bands, slots, side, _ = blocks.shape
    cells = bands * side
    receives, sends = w is not None, x is not None
    most = bands * (slots - 1) + GROUP
    state = jax.ShapeDtypeStruct((chains, cells), jnp.float32)
    parcel = jax.ShapeDtypeStruct((cap, chains, side), jnp.float32)
    in_specs, args = [SMEM, ANY], [meta, blocks]
    out_shape = []
    scratch = [
        pltpu.VMEM((most, side, side), jnp.float32),
        pltpu.VMEM((most, 2 * side, side), jnp.bfloat16),
        pltpu.SemaphoreType.DMA((most,)),
        pltpu.SemaphoreType.DMA((8,)),
    ]
    if receives:
        in_specs += [SMEM, ANY, ANY]
        args += [coef, w, halo]
        out_shape += [state]
        scratch += [
            pltpu.VMEM((chains, cells + side), jnp.float32),
            pltpu.VMEM((cap, chains, side), jnp.float32),
            pltpu.VMEM((cap + 1, 2 * chains, side), jnp.bfloat16),
        ]
    if receives and sends:
        in_specs += [SMEM, ANY]
        args += [given, carry]
        out_shape += [state, parcel]
        if ends:
            out_shape += [jax.ShapeDtypeStruct((1, cells), jnp.float32)]
        scratch += [
            pltpu.VMEM((cap, chains, side), jnp.float32),
            pltpu.VMEM((cap, chains, side), jnp.float32),
        ]
    if sends:
        in_specs += [ANY]
        args += [x]
        out_shape += [parcel]
        scratch += [
            pltpu.VMEM((chains, cells), jnp.float32),
            pltpu.VMEM((2 * chains, cells + side), jnp.bfloat16),
            pltpu.VMEM((cap + 1, chains, side), jnp.float32),
        ]
    return pl.pallas_call(
        functools.partial(
            far_kernel, bands=bands, side=side, cap=cap, x_row=x_row, scale_at=scale_at,
            receives=receives, sends=sends, ends=ends,
        ),
        out_shape=out_shape,
        in_specs=in_specs,
        out_specs=[VMEM if o.shape == (1, cells) else ANY for o in out_shape],
        scratch_shapes=scratch,
        compiler_params=PARAMS,
        cost_estimate=COST,
        name="far",
    )(*args)


def pack_call(given, x, chains, part, cap, side):
    return pl.pallas_call(
        functools.partial(pack_kernel, cap=cap),
        out_shape=jax.ShapeDtypeStruct((cap, chains, side), jnp.float32),
        grid=(1,),
        in_specs=[SMEM, pl.BlockSpec((chains, x.shape[1]), lambda i: (part, 0))],
        out_specs=pl.BlockSpec((cap, chains, side), lambda i: (0, 0, 0)),
        compiler_params=PARAMS,
        cost_estimate=COST,
        name="pack",
    )(given, x)


def end_call(given, coef, v, carry, offset, earlier, part, scale_at):
    cap, chains, side = carry.shape
    cells = v.shape[1]
    in_specs = [
        SMEM,
        SMEM,
        pl.BlockSpec((chains, cells), lambda i: (0, 0)),
        pl.BlockSpec((cap, chains, side), lambda i: (0, 0, 0)),
        pl.BlockSpec((chains, cells), lambda i: (part, 0)),
    ]
    args = [given, coef, v, carry, offset]
    if earlier is not None:
        in_specs.append(ANY)
        args.append(earlier)
    return pl.pallas_call(
        functools.partial(end_kernel, cap=cap, scale_at=scale_at),
        out_shape=[
            jax.ShapeDtypeStruct(offset.shape, jnp.float32),
            jax.ShapeDtypeStruct((chains, side), jnp.float32),
        ],
        grid=(1,),
        in_specs=in_specs,
        out_specs=[
            pl.BlockSpec((chains, cells), lambda i: (part, 0)),
            pl.BlockSpec((chains, side), lambda i: (0, 0)),
        ],
        scratch_shapes=[pltpu.VMEM((chains, 8 * side), jnp.float32)],
        input_output_aliases={} if earlier is None else {5: 0},
        compiler_params=PARAMS,
        cost_estimate=COST,
        name="end",
    )(*args)


def spread_call(start, x, total_start, total_end, side, chain_total):
    return pl.pallas_call(
        functools.partial(spread_kernel, side=side, chain_total=chain_total),
        out_shape=[
            jax.ShapeDtypeStruct(start.shape, jnp.float32),
            jax.ShapeDtypeStruct(start.shape, jnp.float32),
            jax.ShapeDtypeStruct((start.shape[0], side), jnp.float32),
        ],
        in_specs=[VMEM] * (3 + len(x)),
        out_specs=[VMEM] * 3,
        scratch_shapes=[pltpu.VMEM((start.shape[0], 4 * side), jnp.float32)],
        compiler_params=PARAMS,
        cost_estimate=COST,
        name="spread",
    )(start, *x, total_start, total_end)


def summed_over_rows(value):
    count = lax.axis_size("rows")
    reach = 1
    while reach < count:
        radix = 2 if reach == 1 else 4 if count % (4 * reach) == 0 else 2
        own = value
        for k in range(1, radix):
            pairs = [(source, source ^ (k * reach)) for source in range(count)]
            value = value + lax.ppermute(own, "rows", pairs)
        reach *= radix
    return value


def on_device(
    start, momenta, observed, precision_obs, blocks, block_cols, block_count, step_size, trajectory
):
    bands, slots, side, _ = blocks.shape
    cells = bands * side
    local_chains = start.shape[0]
    chains = local_chains // CHUNKS
    nblocks = bands * lax.axis_size("rows")
    all_cells = cells * lax.axis_size("rows")
    chain_total = local_chains * lax.axis_size("grp")
    first = (lax.axis_index("rows") * bands).astype(jnp.int32).reshape(1)
    meta, near_list = pl.pallas_call(
        functools.partial(plan_kernel, bands=bands, slots=slots, nblocks=nblocks),
        out_shape=[jax.ShapeDtypeStruct((META,), jnp.int32)] * 2,
        in_specs=[SMEM, SMEM, SMEM],
        out_specs=[SMEM, SMEM],
        scratch_shapes=[pltpu.SMEM((bands + 8,), jnp.int32)],
        name="plan",
    )(first, block_cols.T, block_count)
    given = passed_along(meta[:ROW_AT], 1)
    step_len = step_size[0]
    coef = jnp.stack([step_len / 2, step_len, step_len])
    seen = observed.reshape(1, cells)
    weight = precision_obs.reshape(1, cells)
    parts = range(CHUNKS)

    def two_steps(cap, start, momenta):
        far = functools.partial(far_call, meta, given, coef, blocks)

        def near(x, v, x_row, v_row, scale_at):
            return near_call(
                near_list, coef, x, v, seen, weight, blocks, chains, x_row, v_row, scale_at
            )

        x, v, w, flight = [start] * CHUNKS, [momenta] * CHUNKS, [], []
        rows = [h * chains for h in parts]
        for h in parts:
            (carry,) = far(start, None, None, None, chains, rows[h], 0, cap)
            halo = pack_call(given, start, chains, h, cap, side)
            flight.append((passed_along(halo, -1), passed_along(carry, 1)))
        for h in parts:
            w.append(near(start, momenta, rows[h], rows[h], 0))
        w = list(lax.optimization_barrier(tuple(w)))
        columns = []
        for turn in range(2):
            for h in parts:
                halo, carry = flight[h]
                v[h], x[h], halo, *column, carry = far(
                    x[h], w[h], halo, carry, chains, rows[h], turn, cap, turn == 1
                )
                columns += column
                flight[h] = (passed_along(halo, -1), passed_along(carry, 1))
                rows[h] = 0
                w[h] = near(x[h], v[h], 0, 0, 1 - turn)
                w = list(lax.optimization_barrier(tuple(w)))
        total_start, total_end = lax.psum(
            (jnp.sum(start, axis=0, keepdims=True), sum(columns[1:], columns[0])), "grp"
        )
        momentum, dots = None, []
        for h in parts:
            halo, carry = flight[h]
            if h < CHUNKS - 1:
                halo, carry = lax.optimization_barrier((halo, carry))
            (v[h],) = far(None, w[h], halo, None, chains, 0, 0, cap)
            if h == 0:
                v[0], total_start, total_end = lax.optimization_barrier(
                    (v[0], total_start, total_end)
                )
                position, offset, gain = spread_call(
                    start, x, total_start, total_end, side, chain_total
                )
            momentum, dot = end_call(given, coef, v[h], carry, offset, momentum, h, 0)
            dots.append(dot)
            if h < CHUNKS - 1:
                w[h + 1], momentum = lax.optimization_barrier((w[h + 1], momentum))
        over = jnp.broadcast_to((meta[1] > cap).astype(jnp.float32), (8, side))
        sums = summed_over_rows(jnp.concatenate([gain, *dots, over], axis=0))
        per_chain = jnp.sum(sums, axis=1)
        spread = per_chain[:local_chains]
        inner = per_chain[local_chains : 2 * local_chains]
        chees = trajectory * (spread / all_cells) * (inner / all_cells)
        return sums[-1, 0], position, momentum, chees

    cap = min(CAP, bands)
    results = two_steps(cap, start, momenta)
    if cap < bands:
        results = lax.while_loop(
            lambda state: state[0] > 0.0,
            lambda state: two_steps(
                bands,
                jnp.where(state[0] > 0.0, start, 0.0),
                jnp.where(state[0] > 0.0, momenta, 0.0),
            ),
            results,
        )
    return tuple(results[1:])


def solution(mesh):
    placed = (
        P("grp", "rows"),
        P("grp", "rows"),
        P("rows"),
        P("rows"),
        P("rows", None, None, None),
        P("rows", None),
        P("rows"),
        P(),
        P("grp"),
    )
    return jax.shard_map(
        on_device,
        mesh=mesh,
        in_specs=placed,
        out_specs=(P("grp", "rows"), P("grp", "rows"), P("grp")),
        check_vma=False,
    )
```

```python
import functools

import jax
import jax.numpy as jnp
from jax import lax
from jax.experimental import pallas as pl
from jax.experimental.pallas import tpu as pltpu
from jax.sharding import PartitionSpec as P

CHUNKS = 2
GROUP = 12
CAP = 46
VMEM_LIMIT = 60 * 2**20
LIST_AT = 8
ROW_AT = 128
SLOT_AT = 384
PLACE_AT = 640
META = 896

NT = (((1,), (1,)), ((), ()))
NN = (((1,), (0,)), ((), ()))


def passed_along(value, steps):
    count = lax.axis_size("rows")
    pairs = [(source, (source + steps) % count) for source in range(count)]
    return lax.ppermute(value, "rows", pairs)


def product(left, right, dims):
    return lax.dot_general(left, right, dims, preferred_element_type=jnp.float32)


def halves(value):
    high = value.astype(jnp.bfloat16)
    low = (value - high.astype(jnp.float32)).astype(jnp.bfloat16)
    return high, low


def doubled(own, chains):
    top = jnp.concatenate([own[:chains], jnp.zeros_like(own[:chains])], axis=0)
    return jnp.concatenate([own, top], axis=1)


def folded_up(value, chains, side):
    return value[:chains, :side] + (value[:chains, side:] + value[chains:, :side])


def stacked(block):
    high, low = halves(block)
    return jnp.concatenate([high, low], axis=0)


def local_column(cols_ref, r, s, first, bands, nblocks):
    raw = cols_ref[s, r] - first
    return jnp.where(raw < 0, raw + nblocks, raw)


def tiles_kernel(first_ref, cols_ref, count_ref, tiles_ref, place_ref, *, bands, slots, nblocks):
    first = first_ref[0]

    def clear(i, _):
        place_ref[i] = 0
        return 0

    lax.fori_loop(0, bands, clear, 0, unroll=8)

    def by_row(r, _):
        live = count_ref[r]
        for s in range(1, slots):
            col = local_column(cols_ref, r, s, first, bands, nblocks)
            far = jnp.logical_and(s < live, col >= bands)
            place_ref[jnp.where(far, col - bands, bands)] = 1
        return 0

    lax.fori_loop(0, bands, by_row, 0, unroll=4)

    def by_tile(m, tiles):
        tiles_ref[LIST_AT + tiles] = m
        used = place_ref[m]
        place_ref[m] = tiles
        return tiles + used

    tiles_ref[1] = lax.fori_loop(0, bands, by_tile, jnp.int32(0), unroll=4)


def edges_kernel(
    first_ref, cols_ref, count_ref, place_ref, far_ref, near_ref, *, bands, slots, nblocks
):
    first = first_ref[0]

    def by_row(r, counts):
        edges, nears = counts
        live = count_ref[r]
        for s in range(1, slots):
            col = local_column(cols_ref, r, s, first, bands, nblocks)
            is_live = s < live
            near = jnp.logical_and(is_live, col < bands)
            far = jnp.logical_and(is_live, col >= bands)
            far_ref[ROW_AT + edges] = r
            far_ref[SLOT_AT + edges] = s
            far_ref[PLACE_AT + edges] = place_ref[jnp.where(far, col - bands, 0)]
            near_ref[ROW_AT + nears] = r
            near_ref[SLOT_AT + nears] = s
            near_ref[PLACE_AT + nears] = col
            edges = edges + far.astype(jnp.int32)
            nears = nears + near.astype(jnp.int32)
        return edges, nears

    edges, nears = lax.fori_loop(0, bands, by_row, (jnp.int32(0), jnp.int32(0)), unroll=4)
    far_ref[0] = edges
    near_ref[0] = nears
    for i in range(GROUP):
        far_ref[ROW_AT + edges + i] = bands
        far_ref[SLOT_AT + edges + i] = 0
        far_ref[PLACE_AT + edges + i] = bands
        near_ref[ROW_AT + nears + i] = bands
        near_ref[SLOT_AT + nears + i] = 0
        near_ref[PLACE_AT + nears + i] = bands


def near_kernel(
    list_ref, coef_ref, x_hbm, v_hbm, seen_ref, weight_ref, blocks_hbm, out_hbm,
    x_buf, v_buf, diag, raw, split, total, sems, diag_sems, sem_of,
    *, bands, side, x_row, v_row, scale_at,
):
    chains = x_buf.shape[0]
    cells = bands * side
    edges = list_ref[0]
    groups = lax.div(edges + GROUP - 1, GROUP)
    pieces = diag_sems.shape[0]
    piece = bands // pieces

    def tile_at(index):
        return pl.ds(pl.multiple_of(index * side, side), side)

    get_x = pltpu.make_async_copy(x_hbm.at[pl.ds(x_row, chains)], x_buf, sems.at[0])
    get_v = pltpu.make_async_copy(v_hbm.at[pl.ds(v_row, chains)], v_buf, sems.at[1])
    put_w = pltpu.make_async_copy(v_buf, out_hbm, sems.at[2])

    def fetch_diag(p):
        rows = pl.ds(p * piece, piece)
        return pltpu.make_async_copy(blocks_hbm.at[rows, 0], diag.at[rows], diag_sems.at[p])

    def fetch(e):
        return pltpu.make_async_copy(
            blocks_hbm.at[list_ref[ROW_AT + e], list_ref[SLOT_AT + e]], raw.at[e], sem_of.at[e]
        )

    get_x.start()
    for p in range(pieces):
        fetch_diag(p).start()

    def start_fetch(e, _):
        fetch(e).start()
        return 0

    lax.fori_loop(0, edges, start_fetch, 0)
    get_v.start()
    get_x.wait()
    high, low = halves(x_buf[...])
    split[:chains, :cells] = high
    split[chains:, :cells] = low
    split[:, cells:] = jnp.zeros((2 * chains, side), jnp.bfloat16)
    total[:, cells:] = jnp.zeros((chains, side), jnp.float32)

    def diag_piece(p, _):
        fetch_diag(p).wait()
        for i in range(piece):
            r = p * piece + i
            up = product(split[:, tile_at(r)], stacked(diag[r]), NT)
            total[:, tile_at(r)] = folded_up(up, chains, side)
        return 0

    lax.fori_loop(0, pieces, diag_piece, 0)

    def group(g, _):
        base = g * GROUP
        for i in range(GROUP):

            @pl.when(base + i < edges)
            def _():
                fetch(base + i).wait()

        ups, downs, rows, cols = [], [], [], []
        for i in range(GROUP):
            rows.append(list_ref[ROW_AT + base + i])
            cols.append(list_ref[PLACE_AT + base + i])
            value = stacked(raw[base + i])
            ups.append(folded_up(product(split[:, tile_at(cols[i])], value, NT), chains, side))
            down = product(doubled(split[:, tile_at(rows[i])], chains), value, NN)
            downs.append(down[:chains] + down[chains:])
        for i in range(GROUP):
            total[:, tile_at(rows[i])] += ups[i]
            total[:, tile_at(cols[i])] += downs[i]
        return 0

    lax.fori_loop(0, groups, group, 0)
    get_v.wait()
    pull = total[:, :cells] + weight_ref[...] * (x_buf[...] - seen_ref[...])
    v_buf[...] = v_buf[...] - coef_ref[scale_at] * pull
    put_w.start()
    put_w.wait()


def far_kernel(
    *refs, bands, side, cap, x_row, scale_at, receives, sends, ends, dots=False,
    out_row=0, follows=False, step_at=2,
):
    refs = list(refs)

    def take(count):
        taken = refs[:count]
        del refs[:count]
        return taken

    (meta_ref, blocks_hbm) = take(2)
    if receives:
        coef_ref, w_hbm, halo_hbm = take(3)
        given_ref, carry_hbm = take(2)
    if sends:
        (x_hbm,) = take(1)
    if ends:
        (before_ref,) = take(1)
    if dots:
        (off_hbm,) = take(1)
    if follows:
        take(1)
    if receives:
        (v_out,) = take(1)
    if dots:
        (dot_out,) = take(1)
    if receives and sends:
        x_out, halo_out = take(2)
    if ends:
        (column_out,) = take(1)
    if sends:
        (carry_out,) = take(1)
    raw, both, sem_of, sems = take(4)
    if receives:
        vel, halo_buf, halo_split, carry_buf = take(4)
    if receives and sends:
        (packed_buf,) = take(1)
    if dots:
        off_buf, sums = take(2)
    if sends:
        x_buf, split, sum_carry = take(3)
    chains = (vel if receives else x_buf).shape[0]
    cells = bands * side
    edges = meta_ref[0]
    groups = lax.div(edges + GROUP - 1, GROUP)

    def tile_at(index):
        return pl.ds(pl.multiple_of(index * side, side), side)

    def fetch(e):
        return pltpu.make_async_copy(
            blocks_hbm.at[meta_ref[ROW_AT + e], meta_ref[SLOT_AT + e]], raw.at[e], sem_of.at[e]
        )

    def start_fetch(e, _):
        fetch(e).start()
        return 0

    def await_group(base):
        for i in range(GROUP):

            @pl.when(base + i < edges)
            def _():
                fetch(base + i).wait()

    if sends:
        get_x = pltpu.make_async_copy(x_hbm.at[pl.ds(x_row, chains)], x_buf, sems.at[0])
    if receives:
        get_halo = pltpu.make_async_copy(halo_hbm, halo_buf, sems.at[1])
        get_w = pltpu.make_async_copy(w_hbm, vel.at[:, pl.ds(0, cells)], sems.at[2])
        v_target = v_out if sends else v_out.at[pl.ds(out_row, chains)]
        put_v = pltpu.make_async_copy(vel.at[:, pl.ds(0, cells)], v_target, sems.at[3])
        get_halo.start()
        get_w.start()
    if sends and not receives:
        get_x.start()
    lax.fori_loop(0, edges, start_fetch, 0)
    if receives:
        get_carry = pltpu.make_async_copy(carry_hbm, carry_buf, sems.at[4])
        get_carry.start()
    if receives and sends:
        get_x.start()
    if dots:
        get_off = pltpu.make_async_copy(off_hbm, off_buf, sems.at[5])
        get_off.start()

    if receives:
        scale = coef_ref[scale_at]
        get_halo.wait()
        high, low = halves(halo_buf[...])
        halo_split[:cap, :chains] = high
        halo_split[:cap, chains:] = low
        halo_split[cap] = jnp.zeros((2 * chains, side), jnp.bfloat16)
        get_w.wait()
        vel[:, cells:] = jnp.zeros((chains, side), jnp.float32)

        def up_group(g, _):
            base = g * GROUP
            await_group(base)
            sums, rows = [], []
            for i in range(GROUP):
                rows.append(meta_ref[ROW_AT + base + i])
                value = stacked(raw[base + i])
                if sends:
                    both[base + i] = value
                place = jnp.minimum(meta_ref[PLACE_AT + base + i], cap)
                sums.append(folded_up(product(halo_split[place], value, NT), chains, side))
            for i in range(GROUP):
                vel[:, tile_at(rows[i])] -= scale * sums[i]
            return 0

        lax.fori_loop(0, groups, up_group, 0)
    if receives:
        given = jnp.minimum(given_ref[1], cap)
        get_carry.wait()

        def add_carry(k, _):
            vel[:, tile_at(given_ref[LIST_AT + k])] -= scale * carry_buf[k]
            return 0

        lax.fori_loop(0, given, add_carry, 0)
    if receives:
        put_v.start()
    if dots:
        get_off.wait()
        dot_out[...] = chain_sums(lambda part: vel[:, part] * off_buf[:, part], sums, cells)
    if sends:
        get_x.wait()
    if receives and sends:
        x_buf[...] += coef_ref[step_at] * vel[:, :cells]
        put_x = pltpu.make_async_copy(x_buf, x_out, sems.at[5])
        put_x.start()
        if ends:
            column_out[:, :cells] = before_ref[:, :cells]
            column_out[:, cells:] = before_ref[:, cells:] + jnp.sum(
                x_buf[...], axis=0, keepdims=True
            )

        def pack(k, _):
            packed_buf[k] = x_buf[:, tile_at(given_ref[LIST_AT + k])]
            return 0

        lax.fori_loop(0, given, pack, 0)
        put_halo = pltpu.make_async_copy(packed_buf, halo_out, sems.at[6])
        put_halo.start()
    if sends:
        high, low = halves(x_buf[...])
        split[:chains, :cells] = high
        split[chains:, :cells] = low
        split[:, cells:] = jnp.zeros((2 * chains, side), jnp.bfloat16)
        sum_carry[...] = jnp.zeros_like(sum_carry)

        def down_group(g, _):
            base = g * GROUP
            if not receives:
                await_group(base)
            sums, places = [], []
            for i in range(GROUP):
                row = meta_ref[ROW_AT + base + i]
                places.append(jnp.minimum(meta_ref[PLACE_AT + base + i], cap))
                value = both[base + i] if receives else stacked(raw[base + i])
                down = product(doubled(split[:, tile_at(row)], chains), value, NN)
                sums.append(down[:chains] + down[chains:])
            for i in range(GROUP):
                sum_carry[places[i]] += sums[i]
            return 0

        lax.fori_loop(0, groups, down_group, 0)
        put_carry = pltpu.make_async_copy(sum_carry.at[pl.ds(0, cap)], carry_out, sems.at[7])
        put_carry.start()
        put_carry.wait()
    if receives and sends:
        put_x.wait()
        put_halo.wait()
    if receives:
        put_v.wait()


def pack_kernel(given_ref, x_ref, out_ref, *, cap):
    side = out_ref.shape[2]

    def pack(k, _):
        tile = pl.ds(pl.multiple_of(given_ref[LIST_AT + k] * side, side), side)
        out_ref[k] = x_ref[:, tile]
        return 0

    lax.fori_loop(0, jnp.minimum(given_ref[1], cap), pack, 0)


def chain_sums(piece, sums, cells):
    wide = sums.shape[1]
    side = wide // 4
    sums[...] = jnp.zeros_like(sums)

    def add(i, _):
        sums[...] += piece(pl.ds(pl.multiple_of(i * wide, wide), wide))
        return 0

    lax.fori_loop(0, cells // wide, add, 0, unroll=2)
    lanes = sum(sums[:, i * side : (i + 1) * side] for i in range(4))
    return lax.dot_general(
        jnp.ones((8, side), jnp.float32), lanes, NT,
        precision=lax.Precision.HIGHEST, preferred_element_type=jnp.float32,
    )


def spread_kernel(
    start_ref, x0_ref, x1_ref, v_ref, *refs, chain_total
):
    *column_refs, position_ref, offset_ref, gain_ref, dot_ref, sums, means = refs
    chains = x0_ref.shape[0]
    cells = start_ref.shape[1]
    means[...] = sum(ref[...] for ref in column_refs) / chain_total
    upper = pl.ds(0, chains)
    lower = pl.ds(chains, chains)

    def ends(part):
        mean_start = means[:, part]
        mean_end = means[:, pl.ds(pl.multiple_of(cells + part.start, 128), part.size)]
        x0 = x0_ref[:, part]
        x1 = x1_ref[:, part]
        position_ref[upper, part] = x0
        position_ref[lower, part] = x1
        off_start = start_ref[:, part] - mean_start
        off1 = x1 - mean_end
        offset_ref[:, part] = off1
        off_end = jnp.concatenate([x0 - mean_end, off1], axis=0)
        return off_end * off_end - off_start * off_start

    gain_ref[...] = chain_sums(ends, sums, cells)

    def first_dot(part):
        mean_end = means[:, pl.ds(pl.multiple_of(cells + part.start, 128), part.size)]
        return (x0_ref[:, part] - mean_end) * v_ref[:, part]

    dot_ref[...] = chain_sums(first_dot, sums.at[upper], cells)


SMEM = pl.BlockSpec(memory_space=pltpu.SMEM)
VMEM = pl.BlockSpec(memory_space=pltpu.VMEM)
ANY = pl.BlockSpec(memory_space=pl.ANY)
PARAMS = pltpu.CompilerParams(vmem_limit_bytes=VMEM_LIMIT)
COST = pl.CostEstimate(flops=1000, bytes_accessed=1000, transcendentals=0)


def near_call(near_list, coef, x, v, seen, weight, blocks, chains, x_row, v_row, scale_at):
    bands, slots, side, _ = blocks.shape
    cells = bands * side
    most = bands * (slots - 1) + GROUP
    pieces = 8 if bands % 8 == 0 else 1
    return pl.pallas_call(
        functools.partial(
            near_kernel, bands=bands, side=side, x_row=x_row, v_row=v_row, scale_at=scale_at
        ),
        out_shape=jax.ShapeDtypeStruct((chains, cells), jnp.float32),
        in_specs=[SMEM, SMEM, ANY, ANY, VMEM, VMEM, ANY],
        out_specs=ANY,
        scratch_shapes=[
            pltpu.VMEM((chains, cells), jnp.float32),
            pltpu.VMEM((chains, cells), jnp.float32),
            pltpu.VMEM((bands, side, side), jnp.float32),
            pltpu.VMEM((most, side, side), jnp.float32),
            pltpu.VMEM((2 * chains, cells + side), jnp.bfloat16),
            pltpu.VMEM((chains, cells + side), jnp.float32),
            pltpu.SemaphoreType.DMA((3,)),
            pltpu.SemaphoreType.DMA((pieces,)),
            pltpu.SemaphoreType.DMA((most,)),
        ],
        compiler_params=PARAMS,
        cost_estimate=COST,
        name="near",
    )(near_list, coef, x, v, seen, weight, blocks)


def far_call(
    meta, given, coef, blocks, x, w, halo, carry, chains, x_row, scale_at, cap, before=None,
    offset=None, earlier=None, out_row=0,
):
    bands, slots, side, _ = blocks.shape
    cells = bands * side
    receives, sends = w is not None, x is not None
    ends, dots, follows = before is not None, offset is not None, earlier is not None
    most = bands * (slots - 1) + GROUP
    state = jax.ShapeDtypeStruct((chains, cells), jnp.float32)
    parcel = jax.ShapeDtypeStruct((cap, chains, side), jnp.float32)
    in_specs, args = [SMEM, ANY], [meta, blocks]
    out_shape, out_specs = [], []
    scratch = [
        pltpu.VMEM((most, side, side), jnp.float32),
        pltpu.VMEM((most, 2 * side, side), jnp.bfloat16),
        pltpu.SemaphoreType.DMA((most,)),
        pltpu.SemaphoreType.DMA((8,)),
    ]
    if receives:
        in_specs += [SMEM, ANY, ANY, SMEM, ANY]
        args += [coef, w, halo, given, carry]
        full = jax.ShapeDtypeStruct((CHUNKS * chains, cells), jnp.float32)
        out_shape += [state if sends else full]
        out_specs += [ANY]
        scratch += [
            pltpu.VMEM((chains, cells + side), jnp.float32),
            pltpu.VMEM((cap, chains, side), jnp.float32),
            pltpu.VMEM((cap + 1, 2 * chains, side), jnp.bfloat16),
            pltpu.VMEM((cap, chains, side), jnp.float32),
        ]
    if receives and sends:
        out_shape += [state, parcel]
        out_specs += [ANY, ANY]
        if ends:
            out_shape += [jax.ShapeDtypeStruct(before.shape, jnp.float32)]
            out_specs += [VMEM]
        scratch += [pltpu.VMEM((cap, chains, side), jnp.float32)]
    if dots:
        in_specs += [ANY]
        args += [offset]
        out_shape += [jax.ShapeDtypeStruct((8, chains), jnp.float32)]
        out_specs += [VMEM]
        scratch += [
            pltpu.VMEM((chains, cells), jnp.float32),
            pltpu.VMEM((chains, 4 * side), jnp.float32),
        ]
    if sends:
        in_specs += [ANY]
        args += [x]
        out_shape += [parcel]
        out_specs += [ANY]
        scratch += [
            pltpu.VMEM((chains, cells), jnp.float32),
            pltpu.VMEM((2 * chains, cells + side), jnp.bfloat16),
            pltpu.VMEM((cap + 1, chains, side), jnp.float32),
        ]
    if ends:
        in_specs += [VMEM]
        args += [before]
    aliases = {}
    if follows:
        aliases = {len(args): 0}
        in_specs += [ANY]
        args += [earlier]
    return pl.pallas_call(
        functools.partial(
            far_kernel, bands=bands, side=side, cap=cap, x_row=x_row, scale_at=scale_at,
            receives=receives, sends=sends, ends=ends, dots=dots, out_row=out_row,
            follows=follows,
        ),
        out_shape=out_shape,
        in_specs=in_specs,
        out_specs=out_specs,
        scratch_shapes=scratch,
        input_output_aliases=aliases,
        compiler_params=PARAMS,
        cost_estimate=COST,
        name="far",
    )(*args)


def pack_call(given, x, chains, part, cap, side):
    return pl.pallas_call(
        functools.partial(pack_kernel, cap=cap),
        out_shape=jax.ShapeDtypeStruct((cap, chains, side), jnp.float32),
        grid=(1,),
        in_specs=[SMEM, pl.BlockSpec((chains, x.shape[1]), lambda i: (part, 0))],
        out_specs=pl.BlockSpec((cap, chains, side), lambda i: (0, 0, 0)),
        compiler_params=PARAMS,
        cost_estimate=COST,
        name="pack",
    )(given, x)


def spread_call(start, x, v, columns, side, chain_total):
    local_chains, cells = start.shape
    chains = x[0].shape[0]
    return pl.pallas_call(
        functools.partial(spread_kernel, chain_total=chain_total),
        out_shape=[
            jax.ShapeDtypeStruct(start.shape, jnp.float32),
            jax.ShapeDtypeStruct((chains, cells), jnp.float32),
            jax.ShapeDtypeStruct((8, local_chains), jnp.float32),
            jax.ShapeDtypeStruct((8, chains), jnp.float32),
        ],
        grid=(1,),
        in_specs=[VMEM, VMEM, VMEM, pl.BlockSpec((chains, cells), lambda i: (0, 0))]
        + [VMEM] * len(columns),
        out_specs=[VMEM] * 4,
        scratch_shapes=[
            pltpu.VMEM((local_chains, 4 * side), jnp.float32),
            pltpu.VMEM((1, 2 * cells), jnp.float32),
        ],
        compiler_params=PARAMS,
        cost_estimate=COST,
        name="spread",
    )(start, *x, v, *columns)


def shared_over(axis, value):
    count = lax.axis_size(axis)
    shared = [value]
    for k in range(1, count):
        pairs = [(source, (source + k) % count) for source in range(count)]
        shared.append(lax.ppermute(value, axis, pairs))
    return shared


def summed_over(axis, value):
    count = lax.axis_size(axis)
    reach = 1
    while reach < count:
        radix = 4 if count % (4 * reach) == 0 and (reach > 1 or count == 4) else 2
        own = value
        for k in range(1, radix):
            pairs = [(source, source ^ (k * reach)) for source in range(count)]
            value = value + lax.ppermute(own, axis, pairs)
        reach *= radix
    return value


def on_device(
    start, momenta, observed, precision_obs, blocks, block_cols, block_count, step_size, trajectory
):
    bands, slots, side, _ = blocks.shape
    cells = bands * side
    local_chains = start.shape[0]
    chains = local_chains // CHUNKS
    nblocks = bands * lax.axis_size("rows")
    all_cells = cells * lax.axis_size("rows")
    chain_total = local_chains * lax.axis_size("grp")
    first = (lax.axis_index("rows") * bands).astype(jnp.int32).reshape(1)
    plan = (first, block_cols.T, block_count)
    sizes = dict(bands=bands, slots=slots, nblocks=nblocks)
    tiles, places = pl.pallas_call(
        functools.partial(tiles_kernel, **sizes),
        out_shape=[
            jax.ShapeDtypeStruct((ROW_AT,), jnp.int32),
            jax.ShapeDtypeStruct((bands + 8,), jnp.int32),
        ],
        in_specs=[SMEM] * 3,
        out_specs=[SMEM] * 2,
        cost_estimate=COST,
        name="tiles",
    )(*plan)
    given = passed_along(tiles, 1)
    meta, near_list = pl.pallas_call(
        functools.partial(edges_kernel, **sizes),
        out_shape=[jax.ShapeDtypeStruct((META,), jnp.int32)] * 2,
        in_specs=[SMEM] * 4,
        out_specs=[SMEM] * 2,
        cost_estimate=COST,
        name="edges",
    )(*plan, places)
    step_len = step_size[0]
    coef = jnp.stack([step_len / 2, step_len, step_len])
    seen = observed.reshape(1, cells)
    weight = precision_obs.reshape(1, cells)
    parts = range(CHUNKS)
    first_rows = [h * chains for h in parts]

    def near(x, v, x_row, v_row, scale_at):
        return near_call(
            near_list, coef, x, v, seen, weight, blocks, chains, x_row, v_row, scale_at
        )

    def two_steps(cap, start, momenta):
        far = functools.partial(far_call, meta, given, coef, blocks)
        x, v, w, flight = [start] * CHUNKS, [momenta] * CHUNKS, [], []
        rows = list(first_rows)
        edges = meta
        for h in parts:
            halo = pack_call(given, start, chains, h, cap, side)
            edges, halo = lax.optimization_barrier((edges, halo))
            (carry,) = far_call(
                edges, given, coef, blocks, start, None, None, None, chains, rows[h], 0, cap
            )
            flight.append((passed_along(halo, -1), passed_along(carry, 1)))
        for h in parts:
            w.append(near(start, momenta, rows[h], rows[h], 0))
        w = list(lax.optimization_barrier(tuple(w)))
        column = jnp.concatenate(
            [jnp.sum(start, axis=0, keepdims=True), jnp.zeros((1, cells), jnp.float32)], axis=1
        )
        for turn in range(2):
            for h in parts:
                halo, carry = flight[h]
                before = column if turn == 1 else None
                v[h], x[h], halo, *after, carry = far(
                    x[h], w[h], halo, carry, chains, rows[h], turn, cap, before
                )
                if after:
                    (column,) = after
                flight[h] = (passed_along(halo, -1), passed_along(carry, 1))
                rows[h] = 0
                w[h] = near(x[h], v[h], 0, 0, 1 - turn)
                w = list(lax.optimization_barrier(tuple(w)))
        column, w[1] = lax.optimization_barrier((column, w[1]))
        (momentum,) = far(None, w[0], *flight[0], chains, 0, 0, cap)
        position, offset, gain, dot = spread_call(
            start, x, momentum, shared_over("grp", column), side, chain_total
        )
        momentum, last_dot = far(
            None, w[1], *flight[1], chains, 0, 0, cap, None, offset, momentum, chains
        )
        over = jnp.full((8, 8), (tiles[1] > cap).astype(jnp.float32))
        sums = summed_over("rows", jnp.concatenate([gain, dot, last_dot, over], axis=1))[0]
        spread, inner = sums[:local_chains], sums[local_chains : 2 * local_chains]
        chees = trajectory * (spread / all_cells) * (inner / all_cells)
        return sums[-1], position, momentum, chees

    cap = min(CAP, bands)
    results = two_steps(cap, start, momenta)
    if cap < bands:
        results = lax.while_loop(
            lambda state: state[0] > 0.0,
            lambda state: two_steps(
                bands,
                jnp.where(state[0] > 0.0, start, 0.0),
                jnp.where(state[0] > 0.0, momenta, 0.0),
            ),
            results,
        )
    return tuple(results[1:])


def solution(mesh):
    placed = (
        P("grp", "rows"),
        P("grp", "rows"),
        P("rows"),
        P("rows"),
        P("rows", None, None, None),
        P("rows", None),
        P("rows"),
        P(),
        P("grp"),
    )
    return jax.shard_map(
        on_device,
        mesh=mesh,
        in_specs=placed,
        out_specs=(P("grp", "rows"), P("grp", "rows"), P("grp")),
        check_vma=False,
    )
```

```python
import functools

import jax
import jax.numpy as jnp
from jax import lax
from jax.experimental import pallas as pl
from jax.experimental.pallas import tpu as pltpu
from jax.sharding import PartitionSpec as P

CHUNKS = 2
GROUP = 12
CAP = 46
VMEM_LIMIT = 60 * 2**20
LIST_AT = 8
ROW_AT = 128
SLOT_AT = 384
PLACE_AT = 640
META = 896

NT = (((1,), (1,)), ((), ()))
NN = (((1,), (0,)), ((), ()))


def passed_along(value, steps):
    count = lax.axis_size("rows")
    pairs = [(source, (source + steps) % count) for source in range(count)]
    return lax.ppermute(value, "rows", pairs)


def product(left, right, dims):
    return lax.dot_general(left, right, dims, preferred_element_type=jnp.float32)


def halves(value):
    high = value.astype(jnp.bfloat16)
    low = (value - high.astype(jnp.float32)).astype(jnp.bfloat16)
    return high, low


def doubled(own, chains):
    top = jnp.concatenate([own[:chains], jnp.zeros_like(own[:chains])], axis=0)
    return jnp.concatenate([own, top], axis=1)


def folded_up(value, chains, side):
    return value[:chains, :side] + (value[:chains, side:] + value[chains:, :side])


def stacked(block):
    high, low = halves(block)
    return jnp.concatenate([high, low], axis=0)


def local_column(cols_ref, r, s, first, bands, nblocks):
    raw = cols_ref[s, r] - first
    return jnp.where(raw < 0, raw + nblocks, raw)


def tiles_kernel(first_ref, cols_ref, count_ref, tiles_ref, place_ref, *, bands, slots, nblocks):
    first = first_ref[0]

    def clear(i, _):
        place_ref[i] = 0
        return 0

    lax.fori_loop(0, bands, clear, 0, unroll=8)

    def by_row(r, _):
        live = count_ref[r]
        for s in range(1, slots):
            col = local_column(cols_ref, r, s, first, bands, nblocks)
            far = jnp.logical_and(s < live, col >= bands)
            place_ref[jnp.where(far, col - bands, bands)] = 1
        return 0

    lax.fori_loop(0, bands, by_row, 0, unroll=4)

    def by_tile(m, tiles):
        tiles_ref[LIST_AT + tiles] = m
        used = place_ref[m]
        place_ref[m] = tiles
        return tiles + used

    tiles_ref[1] = lax.fori_loop(0, bands, by_tile, jnp.int32(0), unroll=4)


def edges_kernel(
    first_ref, cols_ref, count_ref, place_ref, far_ref, near_ref, *, bands, slots, nblocks
):
    first = first_ref[0]

    def by_row(r, counts):
        edges, nears = counts
        live = count_ref[r]
        for s in range(1, slots):
            col = local_column(cols_ref, r, s, first, bands, nblocks)
            is_live = s < live
            near = jnp.logical_and(is_live, col < bands)
            far = jnp.logical_and(is_live, col >= bands)
            far_ref[ROW_AT + edges] = r
            far_ref[SLOT_AT + edges] = s
            far_ref[PLACE_AT + edges] = place_ref[jnp.where(far, col - bands, 0)]
            near_ref[ROW_AT + nears] = r
            near_ref[SLOT_AT + nears] = s
            near_ref[PLACE_AT + nears] = col
            edges = edges + far.astype(jnp.int32)
            nears = nears + near.astype(jnp.int32)
        return edges, nears

    edges, nears = lax.fori_loop(0, bands, by_row, (jnp.int32(0), jnp.int32(0)), unroll=4)
    far_ref[0] = edges
    near_ref[0] = nears
    for i in range(GROUP):
        far_ref[ROW_AT + edges + i] = bands
        far_ref[SLOT_AT + edges + i] = 0
        far_ref[PLACE_AT + edges + i] = bands
        near_ref[ROW_AT + nears + i] = bands
        near_ref[SLOT_AT + nears + i] = 0
        near_ref[PLACE_AT + nears + i] = bands


def near_kernel(
    list_ref, coef_ref, x_hbm, v_hbm, seen_ref, weight_ref, blocks_hbm, out_hbm,
    x_buf, v_buf, diag, raw, split, total, sems, diag_sems, sem_of,
    *, bands, side, x_row, v_row, scale_at,
):
    chains = x_buf.shape[0]
    cells = bands * side
    edges = list_ref[0]
    groups = lax.div(edges + GROUP - 1, GROUP)
    pieces = diag_sems.shape[0]
    piece = bands // pieces

    def tile_at(index):
        return pl.ds(pl.multiple_of(index * side, side), side)

    get_x = pltpu.make_async_copy(x_hbm.at[pl.ds(x_row, chains)], x_buf, sems.at[0])
    get_v = pltpu.make_async_copy(v_hbm.at[pl.ds(v_row, chains)], v_buf, sems.at[1])
    put_w = pltpu.make_async_copy(v_buf, out_hbm, sems.at[2])

    def fetch_diag(p):
        rows = pl.ds(p * piece, piece)
        return pltpu.make_async_copy(blocks_hbm.at[rows, 0], diag.at[rows], diag_sems.at[p])

    def fetch(e):
        return pltpu.make_async_copy(
            blocks_hbm.at[list_ref[ROW_AT + e], list_ref[SLOT_AT + e]], raw.at[e], sem_of.at[e]
        )

    get_x.start()
    for p in range(pieces):
        fetch_diag(p).start()

    def start_fetch(e, _):
        fetch(e).start()
        return 0

    lax.fori_loop(0, edges, start_fetch, 0)
    get_v.start()
    get_x.wait()
    high, low = halves(x_buf[...])
    split[:chains, :cells] = high
    split[chains:, :cells] = low
    split[:, cells:] = jnp.zeros((2 * chains, side), jnp.bfloat16)
    total[:, cells:] = jnp.zeros((chains, side), jnp.float32)

    def diag_piece(p, _):
        fetch_diag(p).wait()
        for i in range(piece):
            r = p * piece + i
            up = product(split[:, tile_at(r)], stacked(diag[r]), NT)
            total[:, tile_at(r)] = folded_up(up, chains, side)
        return 0

    lax.fori_loop(0, pieces, diag_piece, 0)

    def group(g, _):
        base = g * GROUP
        for i in range(GROUP):

            @pl.when(base + i < edges)
            def _():
                fetch(base + i).wait()

        ups, downs, rows, cols = [], [], [], []
        for i in range(GROUP):
            rows.append(list_ref[ROW_AT + base + i])
            cols.append(list_ref[PLACE_AT + base + i])
            value = stacked(raw[base + i])
            ups.append(folded_up(product(split[:, tile_at(cols[i])], value, NT), chains, side))
            down = product(doubled(split[:, tile_at(rows[i])], chains), value, NN)
            downs.append(down[:chains] + down[chains:])
        for i in range(GROUP):
            total[:, tile_at(rows[i])] += ups[i]
            total[:, tile_at(cols[i])] += downs[i]
        return 0

    lax.fori_loop(0, groups, group, 0)
    get_v.wait()
    pull = total[:, :cells] + weight_ref[...] * (x_buf[...] - seen_ref[...])
    v_buf[...] = v_buf[...] - coef_ref[scale_at] * pull
    put_w.start()
    put_w.wait()


def far_kernel(
    *refs, bands, side, cap, x_row, scale_at, receives, sends, ends, dots=False,
    out_row=0, follows=False, step_at=2,
):
    refs = list(refs)

    def take(count):
        taken = refs[:count]
        del refs[:count]
        return taken

    (meta_ref, blocks_hbm) = take(2)
    if receives:
        coef_ref, w_hbm, halo_hbm = take(3)
        given_ref, carry_hbm = take(2)
    if sends:
        (x_hbm,) = take(1)
    if ends:
        (before_ref,) = take(1)
    if dots:
        (off_hbm,) = take(1)
    if follows:
        take(1)
    if receives:
        (v_out,) = take(1)
    if dots:
        (dot_out,) = take(1)
    if receives and sends:
        x_out, halo_out = take(2)
    if ends:
        (column_out,) = take(1)
    if sends:
        (carry_out,) = take(1)
    raw, both, sem_of, sems = take(4)
    if receives:
        vel, halo_buf, halo_split, carry_buf = take(4)
    if receives and sends:
        (packed_buf,) = take(1)
    if dots:
        off_buf, sums = take(2)
    if sends:
        x_buf, split, sum_carry = take(3)
    chains = (vel if receives else x_buf).shape[0]
    cells = bands * side
    edges = meta_ref[0]
    groups = lax.div(edges + GROUP - 1, GROUP)

    def tile_at(index):
        return pl.ds(pl.multiple_of(index * side, side), side)

    def fetch(e):
        return pltpu.make_async_copy(
            blocks_hbm.at[meta_ref[ROW_AT + e], meta_ref[SLOT_AT + e]], raw.at[e], sem_of.at[e]
        )

    def start_fetch(e, _):
        fetch(e).start()
        return 0

    def await_group(base):
        for i in range(GROUP):

            @pl.when(base + i < edges)
            def _():
                fetch(base + i).wait()

    if sends:
        get_x = pltpu.make_async_copy(x_hbm.at[pl.ds(x_row, chains)], x_buf, sems.at[0])
    if receives:
        get_halo = pltpu.make_async_copy(halo_hbm, halo_buf, sems.at[1])
        get_w = pltpu.make_async_copy(w_hbm, vel.at[:, pl.ds(0, cells)], sems.at[2])
        v_target = v_out if sends else v_out.at[pl.ds(out_row, chains)]
        put_v = pltpu.make_async_copy(vel.at[:, pl.ds(0, cells)], v_target, sems.at[3])
        get_halo.start()
        get_w.start()
    if sends and not receives:
        get_x.start()
    lax.fori_loop(0, edges, start_fetch, 0)
    if receives:
        get_carry = pltpu.make_async_copy(carry_hbm, carry_buf, sems.at[4])
        get_carry.start()
    if receives and sends:
        get_x.start()
    if dots:
        get_off = pltpu.make_async_copy(off_hbm, off_buf, sems.at[5])
        get_off.start()

    if receives:
        scale = coef_ref[scale_at]
        get_halo.wait()
        high, low = halves(halo_buf[...])
        halo_split[:cap, :chains] = high
        halo_split[:cap, chains:] = low
        halo_split[cap] = jnp.zeros((2 * chains, side), jnp.bfloat16)
        get_w.wait()
        vel[:, cells:] = jnp.zeros((chains, side), jnp.float32)

        def up_group(g, _):
            base = g * GROUP
            await_group(base)
            sums, rows = [], []
            for i in range(GROUP):
                rows.append(meta_ref[ROW_AT + base + i])
                value = stacked(raw[base + i])
                if sends:
                    both[base + i] = value
                place = jnp.minimum(meta_ref[PLACE_AT + base + i], cap)
                sums.append(folded_up(product(halo_split[place], value, NT), chains, side))
            for i in range(GROUP):
                vel[:, tile_at(rows[i])] -= scale * sums[i]
            return 0

        lax.fori_loop(0, groups, up_group, 0)
    if receives:
        given = jnp.minimum(given_ref[1], cap)
        get_carry.wait()

        def add_carry(k, _):
            vel[:, tile_at(given_ref[LIST_AT + k])] -= scale * carry_buf[k]
            return 0

        lax.fori_loop(0, given, add_carry, 0)
    if receives:
        put_v.start()
    if dots:
        get_off.wait()
        dot_out[...] = chain_sums(lambda part: vel[:, part] * off_buf[:, part], sums, cells)
    if sends:
        get_x.wait()
    if receives and sends:
        x_buf[...] += coef_ref[step_at] * vel[:, :cells]
        put_x = pltpu.make_async_copy(x_buf, x_out, sems.at[5])
        put_x.start()
        if ends:
            column_out[:, :cells] = before_ref[:, :cells]
            column_out[:, cells:] = before_ref[:, cells:] + jnp.sum(
                x_buf[...], axis=0, keepdims=True
            )

        def pack(k, _):
            packed_buf[k] = x_buf[:, tile_at(given_ref[LIST_AT + k])]
            return 0

        lax.fori_loop(0, given, pack, 0)
        put_halo = pltpu.make_async_copy(packed_buf, halo_out, sems.at[6])
        put_halo.start()
    if sends:
        high, low = halves(x_buf[...])
        split[:chains, :cells] = high
        split[chains:, :cells] = low
        split[:, cells:] = jnp.zeros((2 * chains, side), jnp.bfloat16)
        sum_carry[...] = jnp.zeros_like(sum_carry)

        def down_group(g, _):
            base = g * GROUP
            if not receives:
                await_group(base)
            sums, places = [], []
            for i in range(GROUP):
                row = meta_ref[ROW_AT + base + i]
                places.append(jnp.minimum(meta_ref[PLACE_AT + base + i], cap))
                value = both[base + i] if receives else stacked(raw[base + i])
                down = product(doubled(split[:, tile_at(row)], chains), value, NN)
                sums.append(down[:chains] + down[chains:])
            for i in range(GROUP):
                sum_carry[places[i]] += sums[i]
            return 0

        lax.fori_loop(0, groups, down_group, 0)
        put_carry = pltpu.make_async_copy(sum_carry.at[pl.ds(0, cap)], carry_out, sems.at[7])
        put_carry.start()
        put_carry.wait()
    if receives and sends:
        put_x.wait()
        put_halo.wait()
    if receives:
        put_v.wait()


def pack_kernel(given_ref, x_ref, out_ref, *, cap):
    side = out_ref.shape[2]

    def pack(k, _):
        tile = pl.ds(pl.multiple_of(given_ref[LIST_AT + k] * side, side), side)
        out_ref[k] = x_ref[:, tile]
        return 0

    lax.fori_loop(0, jnp.minimum(given_ref[1], cap), pack, 0)


def chain_sums(piece, sums, cells):
    wide = sums.shape[1]
    side = wide // 4
    sums[...] = jnp.zeros_like(sums)

    def add(i, _):
        sums[...] += piece(pl.ds(pl.multiple_of(i * wide, wide), wide))
        return 0

    lax.fori_loop(0, cells // wide, add, 0, unroll=2)
    lanes = sum(sums[:, i * side : (i + 1) * side] for i in range(4))
    return lax.dot_general(
        jnp.ones((8, side), jnp.float32), lanes, NT,
        precision=lax.Precision.HIGHEST, preferred_element_type=jnp.float32,
    )


def spread_kernel(
    start_ref, x0_ref, x1_ref, v_ref, *refs, chain_total
):
    *column_refs, position_ref, offset_ref, gain_ref, dot_ref, sums, means = refs
    chains = x0_ref.shape[0]
    cells = start_ref.shape[1]
    means[...] = sum(ref[...] for ref in column_refs) / chain_total
    upper = pl.ds(0, chains)
    lower = pl.ds(chains, chains)

    def ends(part):
        mean_start = means[:, part]
        mean_end = means[:, pl.ds(pl.multiple_of(cells + part.start, 128), part.size)]
        x0 = x0_ref[:, part]
        x1 = x1_ref[:, part]
        position_ref[upper, part] = x0
        position_ref[lower, part] = x1
        off_start = start_ref[:, part] - mean_start
        off1 = x1 - mean_end
        offset_ref[:, part] = off1
        off_end = jnp.concatenate([x0 - mean_end, off1], axis=0)
        return off_end * off_end - off_start * off_start

    gain_ref[...] = chain_sums(ends, sums, cells)

    def first_dot(part):
        mean_end = means[:, pl.ds(pl.multiple_of(cells + part.start, 128), part.size)]
        return (x0_ref[:, part] - mean_end) * v_ref[:, part]

    dot_ref[...] = chain_sums(first_dot, sums.at[upper], cells)


SMEM = pl.BlockSpec(memory_space=pltpu.SMEM)
VMEM = pl.BlockSpec(memory_space=pltpu.VMEM)
ANY = pl.BlockSpec(memory_space=pl.ANY)
PARAMS = pltpu.CompilerParams(vmem_limit_bytes=VMEM_LIMIT)
COST = pl.CostEstimate(flops=1000, bytes_accessed=1000, transcendentals=0)


def near_call(near_list, coef, x, v, seen, weight, blocks, chains, x_row, v_row, scale_at):
    bands, slots, side, _ = blocks.shape
    cells = bands * side
    most = bands * (slots - 1) + GROUP
    pieces = 8 if bands % 8 == 0 else 1
    return pl.pallas_call(
        functools.partial(
            near_kernel, bands=bands, side=side, x_row=x_row, v_row=v_row, scale_at=scale_at
        ),
        out_shape=jax.ShapeDtypeStruct((chains, cells), jnp.float32),
        in_specs=[SMEM, SMEM, ANY, ANY, VMEM, VMEM, ANY],
        out_specs=ANY,
        scratch_shapes=[
            pltpu.VMEM((chains, cells), jnp.float32),
            pltpu.VMEM((chains, cells), jnp.float32),
            pltpu.VMEM((bands, side, side), jnp.float32),
            pltpu.VMEM((most, side, side), jnp.float32),
            pltpu.VMEM((2 * chains, cells + side), jnp.bfloat16),
            pltpu.VMEM((chains, cells + side), jnp.float32),
            pltpu.SemaphoreType.DMA((3,)),
            pltpu.SemaphoreType.DMA((pieces,)),
            pltpu.SemaphoreType.DMA((most,)),
        ],
        compiler_params=PARAMS,
        cost_estimate=COST,
        name="near",
    )(near_list, coef, x, v, seen, weight, blocks)


def far_call(
    meta, given, coef, blocks, x, w, halo, carry, chains, x_row, scale_at, cap, before=None,
    offset=None, earlier=None, out_row=0,
):
    bands, slots, side, _ = blocks.shape
    cells = bands * side
    receives, sends = w is not None, x is not None
    ends, dots, follows = before is not None, offset is not None, earlier is not None
    most = bands * (slots - 1) + GROUP
    state = jax.ShapeDtypeStruct((chains, cells), jnp.float32)
    parcel = jax.ShapeDtypeStruct((cap, chains, side), jnp.float32)
    in_specs, args = [SMEM, ANY], [meta, blocks]
    out_shape, out_specs = [], []
    scratch = [
        pltpu.VMEM((most, side, side), jnp.float32),
        pltpu.VMEM((most, 2 * side, side), jnp.bfloat16),
        pltpu.SemaphoreType.DMA((most,)),
        pltpu.SemaphoreType.DMA((8,)),
    ]
    if receives:
        in_specs += [SMEM, ANY, ANY, SMEM, ANY]
        args += [coef, w, halo, given, carry]
        full = jax.ShapeDtypeStruct((CHUNKS * chains, cells), jnp.float32)
        out_shape += [state if sends else full]
        out_specs += [ANY]
        scratch += [
            pltpu.VMEM((chains, cells + side), jnp.float32),
            pltpu.VMEM((cap, chains, side), jnp.float32),
            pltpu.VMEM((cap + 1, 2 * chains, side), jnp.bfloat16),
            pltpu.VMEM((cap, chains, side), jnp.float32),
        ]
    if receives and sends:
        out_shape += [state, parcel]
        out_specs += [ANY, ANY]
        if ends:
            out_shape += [jax.ShapeDtypeStruct(before.shape, jnp.float32)]
            out_specs += [VMEM]
        scratch += [pltpu.VMEM((cap, chains, side), jnp.float32)]
    if dots:
        in_specs += [ANY]
        args += [offset]
        out_shape += [jax.ShapeDtypeStruct((8, chains), jnp.float32)]
        out_specs += [VMEM]
        scratch += [
            pltpu.VMEM((chains, cells), jnp.float32),
            pltpu.VMEM((chains, 4 * side), jnp.float32),
        ]
    if sends:
        in_specs += [ANY]
        args += [x]
        out_shape += [parcel]
        out_specs += [ANY]
        scratch += [
            pltpu.VMEM((chains, cells), jnp.float32),
            pltpu.VMEM((2 * chains, cells + side), jnp.bfloat16),
            pltpu.VMEM((cap + 1, chains, side), jnp.float32),
        ]
    if ends:
        in_specs += [VMEM]
        args += [before]
    aliases = {}
    if follows:
        aliases = {len(args): 0}
        in_specs += [ANY]
        args += [earlier]
    return pl.pallas_call(
        functools.partial(
            far_kernel, bands=bands, side=side, cap=cap, x_row=x_row, scale_at=scale_at,
            receives=receives, sends=sends, ends=ends, dots=dots, out_row=out_row,
            follows=follows,
        ),
        out_shape=out_shape,
        in_specs=in_specs,
        out_specs=out_specs,
        scratch_shapes=scratch,
        input_output_aliases=aliases,
        compiler_params=PARAMS,
        cost_estimate=COST,
        name="far",
    )(*args)


def relay_kernel(coef_ref, parcel_ref, out_ref):
    for i in range(3):
        out_ref[i] = coef_ref[i]


def relay_call(coef, parcel):
    return pl.pallas_call(
        relay_kernel,
        out_shape=jax.ShapeDtypeStruct(coef.shape, coef.dtype),
        in_specs=[SMEM, ANY],
        out_specs=SMEM,
        cost_estimate=COST,
        name="relay",
    )(coef, parcel)


def pack_call(given, x, chains, part, cap, side):
    return pl.pallas_call(
        functools.partial(pack_kernel, cap=cap),
        out_shape=jax.ShapeDtypeStruct((cap, chains, side), jnp.float32),
        grid=(1,),
        in_specs=[SMEM, pl.BlockSpec((chains, x.shape[1]), lambda i: (part, 0))],
        out_specs=pl.BlockSpec((cap, chains, side), lambda i: (0, 0, 0)),
        compiler_params=PARAMS,
        cost_estimate=COST,
        name="pack",
    )(given, x)


def spread_call(start, x, v, columns, side, chain_total):
    local_chains, cells = start.shape
    chains = x[0].shape[0]
    return pl.pallas_call(
        functools.partial(spread_kernel, chain_total=chain_total),
        out_shape=[
            jax.ShapeDtypeStruct(start.shape, jnp.float32),
            jax.ShapeDtypeStruct((chains, cells), jnp.float32),
            jax.ShapeDtypeStruct((8, local_chains), jnp.float32),
            jax.ShapeDtypeStruct((8, chains), jnp.float32),
        ],
        grid=(1,),
        in_specs=[VMEM, VMEM, VMEM, pl.BlockSpec((chains, cells), lambda i: (0, 0))]
        + [VMEM] * len(columns),
        out_specs=[VMEM] * 4,
        scratch_shapes=[
            pltpu.VMEM((local_chains, 4 * side), jnp.float32),
            pltpu.VMEM((1, 2 * cells), jnp.float32),
        ],
        compiler_params=PARAMS,
        cost_estimate=COST,
        name="spread",
    )(start, *x, v, *columns)


def shared_over(axis, value):
    count = lax.axis_size(axis)
    shared = [value]
    for k in range(1, count):
        pairs = [(source, (source + k) % count) for source in range(count)]
        shared.append(lax.ppermute(value, axis, pairs))
    return shared


def summed_over(axis, value):
    count = lax.axis_size(axis)
    reach = 1
    while reach < count:
        radix = 4 if count % (4 * reach) == 0 and (reach > 1 or count == 4) else 2
        own = value
        for k in range(1, radix):
            pairs = [(source, source ^ (k * reach)) for source in range(count)]
            value = value + lax.ppermute(own, axis, pairs)
        reach *= radix
    return value


def on_device(
    start, momenta, observed, precision_obs, blocks, block_cols, block_count, step_size, trajectory
):
    bands, slots, side, _ = blocks.shape
    cells = bands * side
    local_chains = start.shape[0]
    chains = local_chains // CHUNKS
    nblocks = bands * lax.axis_size("rows")
    all_cells = cells * lax.axis_size("rows")
    chain_total = local_chains * lax.axis_size("grp")
    first = (lax.axis_index("rows") * bands).astype(jnp.int32).reshape(1)
    plan = (first, block_cols.T, block_count)
    sizes = dict(bands=bands, slots=slots, nblocks=nblocks)
    tiles, places = pl.pallas_call(
        functools.partial(tiles_kernel, **sizes),
        out_shape=[
            jax.ShapeDtypeStruct((ROW_AT,), jnp.int32),
            jax.ShapeDtypeStruct((bands + 8,), jnp.int32),
        ],
        in_specs=[SMEM] * 3,
        out_specs=[SMEM] * 2,
        cost_estimate=COST,
        name="tiles",
    )(*plan)
    given = passed_along(tiles, 1)
    meta, near_list = pl.pallas_call(
        functools.partial(edges_kernel, **sizes),
        out_shape=[jax.ShapeDtypeStruct((META,), jnp.int32)] * 2,
        in_specs=[SMEM] * 4,
        out_specs=[SMEM] * 2,
        cost_estimate=COST,
        name="edges",
    )(*plan, places)
    step_len = step_size[0]
    coef = jnp.stack([step_len / 2, step_len, step_len])
    seen = observed.reshape(1, cells)
    weight = precision_obs.reshape(1, cells)
    parts = range(CHUNKS)
    first_rows = [h * chains for h in parts]

    def near(x, v, x_row, v_row, scale_at):
        return near_call(
            near_list, coef, x, v, seen, weight, blocks, chains, x_row, v_row, scale_at
        )

    def two_steps(cap, start, momenta):
        x, v, w, flight = [start] * CHUNKS, [momenta] * CHUNKS, [], []
        rows = list(first_rows)
        edges = meta
        for h in parts:
            halo = pack_call(given, start, chains, h, cap, side)
            edges, halo = lax.optimization_barrier((edges, halo))
            (carry,) = far_call(
                edges, given, coef, blocks, start, None, None, None, chains, rows[h], 0, cap
            )
            flight.append((passed_along(halo, -1), passed_along(carry, 1)))
        for h in parts:
            w.append(near(start, momenta, rows[h], rows[h], 0))
        w = list(lax.optimization_barrier(tuple(w)))
        column = jnp.concatenate(
            [jnp.sum(start, axis=0, keepdims=True), jnp.zeros((1, cells), jnp.float32)], axis=1
        )
        for turn in range(2):
            for h in parts:
                halo, carry = flight[h]
                before = column if turn == 1 else None
                scales = relay_call(coef, halo) if turn == 0 and h == 0 else coef
                far = functools.partial(far_call, meta, given, scales, blocks)
                v[h], x[h], halo, *after, carry = far(
                    x[h], w[h], halo, carry, chains, rows[h], turn, cap, before
                )
                if after:
                    (column,) = after
                flight[h] = (passed_along(halo, -1), passed_along(carry, 1))
                rows[h] = 0
                w[h] = near(x[h], v[h], 0, 0, 1 - turn)
                w = list(lax.optimization_barrier(tuple(w)))
        column, w[1] = lax.optimization_barrier((column, w[1]))
        (momentum,) = far(None, w[0], *flight[0], chains, 0, 0, cap)
        position, offset, gain, dot = spread_call(
            start, x, momentum, shared_over("grp", column), side, chain_total
        )
        momentum, last_dot = far(
            None, w[1], *flight[1], chains, 0, 0, cap, None, offset, momentum, chains
        )
        over = jnp.full((8, 8), (tiles[1] > cap).astype(jnp.float32))
        sums = summed_over("rows", jnp.concatenate([gain, dot, last_dot, over], axis=1))[0]
        spread, inner = sums[:local_chains], sums[local_chains : 2 * local_chains]
        chees = trajectory * (spread / all_cells) * (inner / all_cells)
        return sums[-1], position, momentum, chees

    cap = min(CAP, bands)
    results = two_steps(cap, start, momenta)
    if cap < bands:
        results = lax.while_loop(
            lambda state: state[0] > 0.0,
            lambda state: two_steps(
                bands,
                jnp.where(state[0] > 0.0, start, 0.0),
                jnp.where(state[0] > 0.0, momenta, 0.0),
            ),
            results,
        )
    return tuple(results[1:])


def solution(mesh):
    placed = (
        P("grp", "rows"),
        P("grp", "rows"),
        P("rows"),
        P("rows"),
        P("rows", None, None, None),
        P("rows", None),
        P("rows"),
        P(),
        P("grp"),
    )
    return jax.shard_map(
        on_device,
        mesh=mesh,
        in_specs=placed,
        out_specs=(P("grp", "rows"), P("grp", "rows"), P("grp")),
        check_vma=False,
    )
```

```python
import functools

import jax
import jax.numpy as jnp
from jax import lax
from jax.experimental import pallas as pl
from jax.experimental.pallas import tpu as pltpu
from jax.sharding import PartitionSpec as P

CHUNKS = 2
GROUP = 12
CAP = 46
VMEM_LIMIT = 60 * 2**20
LIST_AT = 8
ROW_AT = 128
SLOT_AT = 384
PLACE_AT = 640
META = 896

NT = (((1,), (1,)), ((), ()))
NN = (((1,), (0,)), ((), ()))


def passed_along(value, steps):
    count = lax.axis_size("rows")
    pairs = [(source, (source + steps) % count) for source in range(count)]
    return lax.ppermute(value, "rows", pairs)


def product(left, right, dims):
    return lax.dot_general(left, right, dims, preferred_element_type=jnp.float32)


def halves(value):
    high = value.astype(jnp.bfloat16)
    low = (value - high.astype(jnp.float32)).astype(jnp.bfloat16)
    return high, low


def doubled(own, chains):
    top = jnp.concatenate([own[:chains], jnp.zeros_like(own[:chains])], axis=0)
    return jnp.concatenate([own, top], axis=1)


def folded_up(value, chains, side):
    return value[:chains, :side] + (value[:chains, side:] + value[chains:, :side])


def stacked(block):
    high, low = halves(block)
    return jnp.concatenate([high, low], axis=0)


def local_column(cols_ref, r, s, first, bands, nblocks):
    raw = cols_ref[s, r] - first
    return jnp.where(raw < 0, raw + nblocks, raw)


def tiles_kernel(first_ref, cols_ref, count_ref, tiles_ref, place_ref, *, bands, slots, nblocks):
    first = first_ref[0]

    def clear(i, _):
        place_ref[i] = 0
        return 0

    lax.fori_loop(0, bands, clear, 0, unroll=8)

    def by_row(r, _):
        live = count_ref[r]
        for s in range(1, slots):
            col = local_column(cols_ref, r, s, first, bands, nblocks)
            far = jnp.logical_and(s < live, col >= bands)
            place_ref[jnp.where(far, col - bands, bands)] = 1
        return 0

    lax.fori_loop(0, bands, by_row, 0, unroll=4)

    def by_tile(m, tiles):
        tiles_ref[LIST_AT + tiles] = m
        used = place_ref[m]
        place_ref[m] = tiles
        return tiles + used

    tiles_ref[1] = lax.fori_loop(0, bands, by_tile, jnp.int32(0), unroll=4)


def edges_kernel(
    first_ref, cols_ref, count_ref, place_ref, far_ref, near_ref, *, bands, slots, nblocks
):
    first = first_ref[0]

    def by_row(r, counts):
        edges, nears = counts
        live = count_ref[r]
        for s in range(1, slots):
            col = local_column(cols_ref, r, s, first, bands, nblocks)
            is_live = s < live
            near = jnp.logical_and(is_live, col < bands)
            far = jnp.logical_and(is_live, col >= bands)
            far_ref[ROW_AT + edges] = r
            far_ref[SLOT_AT + edges] = s
            far_ref[PLACE_AT + edges] = place_ref[jnp.where(far, col - bands, 0)]
            near_ref[ROW_AT + nears] = r
            near_ref[SLOT_AT + nears] = s
            near_ref[PLACE_AT + nears] = col
            edges = edges + far.astype(jnp.int32)
            nears = nears + near.astype(jnp.int32)
        return edges, nears

    edges, nears = lax.fori_loop(0, bands, by_row, (jnp.int32(0), jnp.int32(0)), unroll=4)
    far_ref[0] = edges
    near_ref[0] = nears
    for i in range(GROUP):
        far_ref[ROW_AT + edges + i] = bands
        far_ref[SLOT_AT + edges + i] = 0
        far_ref[PLACE_AT + edges + i] = bands
        near_ref[ROW_AT + nears + i] = bands
        near_ref[SLOT_AT + nears + i] = 0
        near_ref[PLACE_AT + nears + i] = bands


def near_kernel(
    list_ref, coef_ref, x_hbm, v_hbm, seen_ref, weight_ref, blocks_hbm, out_hbm,
    x_buf, v_buf, diag, raw, split, total, sems, diag_sems, sem_of,
    *, bands, side, x_row, v_row, scale_at,
):
    chains = x_buf.shape[0]
    cells = bands * side
    edges = list_ref[0]
    groups = lax.div(edges + GROUP - 1, GROUP)
    pieces = diag_sems.shape[0]
    piece = bands // pieces

    def tile_at(index):
        return pl.ds(pl.multiple_of(index * side, side), side)

    get_x = pltpu.make_async_copy(x_hbm.at[pl.ds(x_row, chains)], x_buf, sems.at[0])
    get_v = pltpu.make_async_copy(v_hbm.at[pl.ds(v_row, chains)], v_buf, sems.at[1])
    put_w = pltpu.make_async_copy(v_buf, out_hbm, sems.at[2])

    def fetch_diag(p):
        rows = pl.ds(p * piece, piece)
        return pltpu.make_async_copy(blocks_hbm.at[rows, 0], diag.at[rows], diag_sems.at[p])

    def fetch(e):
        return pltpu.make_async_copy(
            blocks_hbm.at[list_ref[ROW_AT + e], list_ref[SLOT_AT + e]], raw.at[e], sem_of.at[e]
        )

    get_x.start()
    for p in range(pieces):
        fetch_diag(p).start()

    def start_fetch(e, _):
        fetch(e).start()
        return 0

    lax.fori_loop(0, edges, start_fetch, 0)
    get_v.start()
    get_x.wait()
    high, low = halves(x_buf[...])
    split[:chains, :cells] = high
    split[chains:, :cells] = low
    split[:, cells:] = jnp.zeros((2 * chains, side), jnp.bfloat16)
    total[:, cells:] = jnp.zeros((chains, side), jnp.float32)

    def diag_piece(p, _):
        fetch_diag(p).wait()
        for i in range(piece):
            r = p * piece + i
            up = product(split[:, tile_at(r)], stacked(diag[r]), NT)
            total[:, tile_at(r)] = folded_up(up, chains, side)
        return 0

    lax.fori_loop(0, pieces, diag_piece, 0)

    def group(g, _):
        base = g * GROUP
        for i in range(GROUP):

            @pl.when(base + i < edges)
            def _():
                fetch(base + i).wait()

        ups, downs, rows, cols = [], [], [], []
        for i in range(GROUP):
            rows.append(list_ref[ROW_AT + base + i])
            cols.append(list_ref[PLACE_AT + base + i])
            value = stacked(raw[base + i])
            ups.append(folded_up(product(split[:, tile_at(cols[i])], value, NT), chains, side))
            down = product(doubled(split[:, tile_at(rows[i])], chains), value, NN)
            downs.append(down[:chains] + down[chains:])
        for i in range(GROUP):
            total[:, tile_at(rows[i])] += ups[i]
            total[:, tile_at(cols[i])] += downs[i]
        return 0

    lax.fori_loop(0, groups, group, 0)
    get_v.wait()
    pull = total[:, :cells] + weight_ref[...] * (x_buf[...] - seen_ref[...])
    v_buf[...] = v_buf[...] - coef_ref[scale_at] * pull
    put_w.start()
    put_w.wait()


def far_kernel(
    *refs, bands, side, cap, x_row, scale_at, receives, sends, ends, dots=False,
    out_row=0, follows=False, step_at=2,
):
    refs = list(refs)

    def take(count):
        taken = refs[:count]
        del refs[:count]
        return taken

    (meta_ref, blocks_hbm) = take(2)
    if receives:
        coef_ref, w_hbm, halo_hbm = take(3)
        given_ref, carry_hbm = take(2)
    if sends:
        (x_hbm,) = take(1)
    if ends:
        (before_ref,) = take(1)
    if dots:
        (off_hbm,) = take(1)
    if follows:
        take(1)
    if receives:
        (v_out,) = take(1)
    if dots:
        (dot_out,) = take(1)
    if receives and sends:
        x_out, halo_out = take(2)
    if ends:
        (column_out,) = take(1)
    if sends:
        (carry_out,) = take(1)
    raw, both, sem_of, sems = take(4)
    if receives:
        vel, halo_buf, halo_split, carry_buf = take(4)
    if receives and sends:
        (packed_buf,) = take(1)
    if dots:
        off_buf, sums = take(2)
    if sends:
        x_buf, split, sum_carry = take(3)
    chains = (vel if receives else x_buf).shape[0]
    cells = bands * side
    edges = meta_ref[0]
    groups = lax.div(edges + GROUP - 1, GROUP)

    def tile_at(index):
        return pl.ds(pl.multiple_of(index * side, side), side)

    def fetch(e):
        return pltpu.make_async_copy(
            blocks_hbm.at[meta_ref[ROW_AT + e], meta_ref[SLOT_AT + e]], raw.at[e], sem_of.at[e]
        )

    def start_fetch(e, _):
        fetch(e).start()
        return 0

    def await_group(base):
        for i in range(GROUP):

            @pl.when(base + i < edges)
            def _():
                fetch(base + i).wait()

    if sends:
        get_x = pltpu.make_async_copy(x_hbm.at[pl.ds(x_row, chains)], x_buf, sems.at[0])
    if receives:
        get_halo = pltpu.make_async_copy(halo_hbm, halo_buf, sems.at[1])
        get_w = pltpu.make_async_copy(w_hbm, vel.at[:, pl.ds(0, cells)], sems.at[2])
        v_target = v_out if sends else v_out.at[pl.ds(out_row, chains)]
        put_v = pltpu.make_async_copy(vel.at[:, pl.ds(0, cells)], v_target, sems.at[3])
        get_halo.start()
        get_w.start()
    if sends and not receives:
        get_x.start()
    lax.fori_loop(0, edges, start_fetch, 0)
    if receives:
        get_carry = pltpu.make_async_copy(carry_hbm, carry_buf, sems.at[4])
        get_carry.start()
    if receives and sends:
        get_x.start()
    if dots:
        off_rows = off_hbm.at[pl.ds(out_row, chains)]
        get_off = pltpu.make_async_copy(off_rows, off_buf, sems.at[5])
        get_off.start()

    if receives:
        scale = coef_ref[scale_at]
        get_halo.wait()
        high, low = halves(halo_buf[...])
        halo_split[:cap, :chains] = high
        halo_split[:cap, chains:] = low
        halo_split[cap] = jnp.zeros((2 * chains, side), jnp.bfloat16)
        get_w.wait()
        vel[:, cells:] = jnp.zeros((chains, side), jnp.float32)

        def up_group(g, _):
            base = g * GROUP
            await_group(base)
            sums, rows = [], []
            for i in range(GROUP):
                rows.append(meta_ref[ROW_AT + base + i])
                value = stacked(raw[base + i])
                if sends:
                    both[base + i] = value
                place = jnp.minimum(meta_ref[PLACE_AT + base + i], cap)
                sums.append(folded_up(product(halo_split[place], value, NT), chains, side))
            for i in range(GROUP):
                vel[:, tile_at(rows[i])] -= scale * sums[i]
            return 0

        lax.fori_loop(0, groups, up_group, 0)
    if receives:
        given = jnp.minimum(given_ref[1], cap)
        get_carry.wait()

        def add_carry(k, _):
            vel[:, tile_at(given_ref[LIST_AT + k])] -= scale * carry_buf[k]
            return 0

        lax.fori_loop(0, given, add_carry, 0)
    if receives:
        put_v.start()
    if dots:
        get_off.wait()
        dot_out[...] = chain_sums(lambda part: vel[:, part] * off_buf[:, part], sums, cells)
    if sends:
        get_x.wait()
    if receives and sends:
        x_buf[...] += coef_ref[step_at] * vel[:, :cells]
        put_x = pltpu.make_async_copy(x_buf, x_out, sems.at[5])
        put_x.start()
        if ends:
            column_out[:, :cells] = before_ref[:, :cells]
            column_out[:, cells:] = before_ref[:, cells:] + jnp.sum(
                x_buf[...], axis=0, keepdims=True
            )

        def pack(k, _):
            packed_buf[k] = x_buf[:, tile_at(given_ref[LIST_AT + k])]
            return 0

        lax.fori_loop(0, given, pack, 0)
        put_halo = pltpu.make_async_copy(packed_buf, halo_out, sems.at[6])
        put_halo.start()
    if sends:
        high, low = halves(x_buf[...])
        split[:chains, :cells] = high
        split[chains:, :cells] = low
        split[:, cells:] = jnp.zeros((2 * chains, side), jnp.bfloat16)
        sum_carry[...] = jnp.zeros_like(sum_carry)

        def down_group(g, _):
            base = g * GROUP
            if not receives:
                await_group(base)
            sums, places = [], []
            for i in range(GROUP):
                row = meta_ref[ROW_AT + base + i]
                places.append(jnp.minimum(meta_ref[PLACE_AT + base + i], cap))
                value = both[base + i] if receives else stacked(raw[base + i])
                down = product(doubled(split[:, tile_at(row)], chains), value, NN)
                sums.append(down[:chains] + down[chains:])
            for i in range(GROUP):
                sum_carry[places[i]] += sums[i]
            return 0

        lax.fori_loop(0, groups, down_group, 0)
        put_carry = pltpu.make_async_copy(sum_carry.at[pl.ds(0, cap)], carry_out, sems.at[7])
        put_carry.start()
        put_carry.wait()
    if receives and sends:
        put_x.wait()
        put_halo.wait()
    if receives:
        put_v.wait()


def pack_kernel(given_ref, x_ref, out_ref, *, cap):
    side = out_ref.shape[2]

    def pack(k, _):
        tile = pl.ds(pl.multiple_of(given_ref[LIST_AT + k] * side, side), side)
        out_ref[k] = x_ref[:, tile]
        return 0

    lax.fori_loop(0, jnp.minimum(given_ref[1], cap), pack, 0)


def chain_sums(piece, sums, cells):
    wide = sums.shape[1]
    side = wide // 4
    sums[...] = jnp.zeros_like(sums)

    def add(i, _):
        sums[...] += piece(pl.ds(pl.multiple_of(i * wide, wide), wide))
        return 0

    lax.fori_loop(0, cells // wide, add, 0, unroll=2)
    lanes = sum(sums[:, i * side : (i + 1) * side] for i in range(4))
    return lax.dot_general(
        jnp.ones((8, side), jnp.float32), lanes, NT,
        precision=lax.Precision.HIGHEST, preferred_element_type=jnp.float32,
    )


def spread_kernel(
    start_ref, x0_ref, x1_ref, *refs, chain_total
):
    *column_refs, position_ref, offset_ref, gain_ref, sums, means = refs
    chains = x0_ref.shape[0]
    cells = start_ref.shape[1]
    means[...] = sum(ref[...] for ref in column_refs) / chain_total
    upper = pl.ds(0, chains)
    lower = pl.ds(chains, chains)

    def ends(part):
        mean_start = means[:, part]
        mean_end = means[:, pl.ds(pl.multiple_of(cells + part.start, 128), part.size)]
        x0 = x0_ref[:, part]
        x1 = x1_ref[:, part]
        position_ref[upper, part] = x0
        position_ref[lower, part] = x1
        off_start = start_ref[:, part] - mean_start
        off_end = jnp.concatenate([x0, x1], axis=0) - mean_end
        offset_ref[:, part] = off_end
        return off_end * off_end - off_start * off_start

    gain_ref[...] = chain_sums(ends, sums, cells)


SMEM = pl.BlockSpec(memory_space=pltpu.SMEM)
VMEM = pl.BlockSpec(memory_space=pltpu.VMEM)
ANY = pl.BlockSpec(memory_space=pl.ANY)
PARAMS = pltpu.CompilerParams(vmem_limit_bytes=VMEM_LIMIT)
COST = pl.CostEstimate(flops=1000, bytes_accessed=1000, transcendentals=0)


def near_call(near_list, coef, x, v, seen, weight, blocks, chains, x_row, v_row, scale_at):
    bands, slots, side, _ = blocks.shape
    cells = bands * side
    most = bands * (slots - 1) + GROUP
    pieces = 8 if bands % 8 == 0 else 1
    return pl.pallas_call(
        functools.partial(
            near_kernel, bands=bands, side=side, x_row=x_row, v_row=v_row, scale_at=scale_at
        ),
        out_shape=jax.ShapeDtypeStruct((chains, cells), jnp.float32),
        in_specs=[SMEM, SMEM, ANY, ANY, VMEM, VMEM, ANY],
        out_specs=ANY,
        scratch_shapes=[
            pltpu.VMEM((chains, cells), jnp.float32),
            pltpu.VMEM((chains, cells), jnp.float32),
            pltpu.VMEM((bands, side, side), jnp.float32),
            pltpu.VMEM((most, side, side), jnp.float32),
            pltpu.VMEM((2 * chains, cells + side), jnp.bfloat16),
            pltpu.VMEM((chains, cells + side), jnp.float32),
            pltpu.SemaphoreType.DMA((3,)),
            pltpu.SemaphoreType.DMA((pieces,)),
            pltpu.SemaphoreType.DMA((most,)),
        ],
        compiler_params=PARAMS,
        cost_estimate=COST,
        name="near",
    )(near_list, coef, x, v, seen, weight, blocks)


def far_call(
    meta, given, coef, blocks, x, w, halo, carry, chains, x_row, scale_at, cap, before=None,
    offset=None, earlier=None, out_row=0,
):
    bands, slots, side, _ = blocks.shape
    cells = bands * side
    receives, sends = w is not None, x is not None
    ends, dots, follows = before is not None, offset is not None, earlier is not None
    most = bands * (slots - 1) + GROUP
    state = jax.ShapeDtypeStruct((chains, cells), jnp.float32)
    parcel = jax.ShapeDtypeStruct((cap, chains, side), jnp.float32)
    in_specs, args = [SMEM, ANY], [meta, blocks]
    out_shape, out_specs = [], []
    scratch = [
        pltpu.VMEM((most, side, side), jnp.float32),
        pltpu.VMEM((most, 2 * side, side), jnp.bfloat16),
        pltpu.SemaphoreType.DMA((most,)),
        pltpu.SemaphoreType.DMA((8,)),
    ]
    if receives:
        in_specs += [SMEM, ANY, ANY, SMEM, ANY]
        args += [coef, w, halo, given, carry]
        full = jax.ShapeDtypeStruct((CHUNKS * chains, cells), jnp.float32)
        out_shape += [state if sends else full]
        out_specs += [ANY]
        scratch += [
            pltpu.VMEM((chains, cells + side), jnp.float32),
            pltpu.VMEM((cap, chains, side), jnp.float32),
            pltpu.VMEM((cap + 1, 2 * chains, side), jnp.bfloat16),
            pltpu.VMEM((cap, chains, side), jnp.float32),
        ]
    if receives and sends:
        out_shape += [state, parcel]
        out_specs += [ANY, ANY]
        if ends:
            out_shape += [jax.ShapeDtypeStruct(before.shape, jnp.float32)]
            out_specs += [VMEM]
        scratch += [pltpu.VMEM((cap, chains, side), jnp.float32)]
    if dots:
        in_specs += [ANY]
        args += [offset]
        out_shape += [jax.ShapeDtypeStruct((8, chains), jnp.float32)]
        out_specs += [VMEM]
        scratch += [
            pltpu.VMEM((chains, cells), jnp.float32),
            pltpu.VMEM((chains, 4 * side), jnp.float32),
        ]
    if sends:
        in_specs += [ANY]
        args += [x]
        out_shape += [parcel]
        out_specs += [ANY]
        scratch += [
            pltpu.VMEM((chains, cells), jnp.float32),
            pltpu.VMEM((2 * chains, cells + side), jnp.bfloat16),
            pltpu.VMEM((cap + 1, chains, side), jnp.float32),
        ]
    if ends:
        in_specs += [VMEM]
        args += [before]
    aliases = {}
    if follows:
        aliases = {len(args): 0}
        in_specs += [ANY]
        args += [earlier]
    return pl.pallas_call(
        functools.partial(
            far_kernel, bands=bands, side=side, cap=cap, x_row=x_row, scale_at=scale_at,
            receives=receives, sends=sends, ends=ends, dots=dots, out_row=out_row,
            follows=follows,
        ),
        out_shape=out_shape,
        in_specs=in_specs,
        out_specs=out_specs,
        scratch_shapes=scratch,
        input_output_aliases=aliases,
        compiler_params=PARAMS,
        cost_estimate=COST,
        name="far",
    )(*args)


def relay_kernel(coef_ref, parcel_ref, out_ref):
    for i in range(3):
        out_ref[i] = coef_ref[i]


def relay_call(coef, parcel):
    return pl.pallas_call(
        relay_kernel,
        out_shape=jax.ShapeDtypeStruct(coef.shape, coef.dtype),
        in_specs=[SMEM, ANY],
        out_specs=SMEM,
        cost_estimate=COST,
        name="relay",
    )(coef, parcel)


def pack_call(given, x, chains, part, cap, side):
    return pl.pallas_call(
        functools.partial(pack_kernel, cap=cap),
        out_shape=jax.ShapeDtypeStruct((cap, chains, side), jnp.float32),
        grid=(1,),
        in_specs=[SMEM, pl.BlockSpec((chains, x.shape[1]), lambda i: (part, 0))],
        out_specs=pl.BlockSpec((cap, chains, side), lambda i: (0, 0, 0)),
        compiler_params=PARAMS,
        cost_estimate=COST,
        name="pack",
    )(given, x)


def spread_call(start, x, columns, side, chain_total):
    local_chains, cells = start.shape
    chains = x[0].shape[0]
    return pl.pallas_call(
        functools.partial(spread_kernel, chain_total=chain_total),
        out_shape=[
            jax.ShapeDtypeStruct(start.shape, jnp.float32),
            jax.ShapeDtypeStruct(start.shape, jnp.float32),
            jax.ShapeDtypeStruct((8, local_chains), jnp.float32),
        ],
        in_specs=[VMEM] * (3 + len(columns)),
        out_specs=[VMEM] * 3,
        scratch_shapes=[
            pltpu.VMEM((local_chains, 4 * side), jnp.float32),
            pltpu.VMEM((1, 2 * cells), jnp.float32),
        ],
        compiler_params=PARAMS,
        cost_estimate=COST,
        name="spread",
    )(start, *x, *columns)


def add_kernel(a_ref, b_ref, out_ref):
    out_ref[...] = a_ref[...] + b_ref[...]


def add_call(a, b):
    return pl.pallas_call(
        add_kernel,
        out_shape=jax.ShapeDtypeStruct(a.shape, a.dtype),
        in_specs=[VMEM, VMEM],
        out_specs=VMEM,
        cost_estimate=COST,
        name="add",
    )(a, b)


def summed_over(axis, value):
    count = lax.axis_size(axis)
    reach = 1
    while reach < count:
        radix = 4 if count % (4 * reach) == 0 and (reach > 1 or count == 4) else 2
        own = value
        for k in range(1, radix):
            pairs = [(source, source ^ (k * reach)) for source in range(count)]
            value = value + lax.ppermute(own, axis, pairs)
        reach *= radix
    return value


def on_device(
    start, momenta, observed, precision_obs, blocks, block_cols, block_count, step_size, trajectory
):
    bands, slots, side, _ = blocks.shape
    cells = bands * side
    local_chains = start.shape[0]
    chains = local_chains // CHUNKS
    nblocks = bands * lax.axis_size("rows")
    all_cells = cells * lax.axis_size("rows")
    chain_total = local_chains * lax.axis_size("grp")
    first = (lax.axis_index("rows") * bands).astype(jnp.int32).reshape(1)
    plan = (first, block_cols.T, block_count)
    sizes = dict(bands=bands, slots=slots, nblocks=nblocks)
    tiles, places = pl.pallas_call(
        functools.partial(tiles_kernel, **sizes),
        out_shape=[
            jax.ShapeDtypeStruct((ROW_AT,), jnp.int32),
            jax.ShapeDtypeStruct((bands + 8,), jnp.int32),
        ],
        in_specs=[SMEM] * 3,
        out_specs=[SMEM] * 2,
        cost_estimate=COST,
        name="tiles",
    )(*plan)
    given = passed_along(tiles, 1)
    meta, near_list = pl.pallas_call(
        functools.partial(edges_kernel, **sizes),
        out_shape=[jax.ShapeDtypeStruct((META,), jnp.int32)] * 2,
        in_specs=[SMEM] * 4,
        out_specs=[SMEM] * 2,
        cost_estimate=COST,
        name="edges",
    )(*plan, places)
    step_len = step_size[0]
    coef = jnp.stack([step_len / 2, step_len, step_len])
    seen = observed.reshape(1, cells)
    weight = precision_obs.reshape(1, cells)
    parts = range(CHUNKS)
    first_rows = [h * chains for h in parts]

    def near(x, v, x_row, v_row, scale_at):
        return near_call(
            near_list, coef, x, v, seen, weight, blocks, chains, x_row, v_row, scale_at
        )

    def two_steps(cap, start, momenta):
        x, v, w, flight = [start] * CHUNKS, [momenta] * CHUNKS, [], []
        rows = list(first_rows)
        edges = meta
        for h in parts:
            halo = pack_call(given, start, chains, h, cap, side)
            edges, halo = lax.optimization_barrier((edges, halo))
            (carry,) = far_call(
                edges, given, coef, blocks, start, None, None, None, chains, rows[h], 0, cap
            )
            flight.append((passed_along(halo, -1), passed_along(carry, 1)))
        for h in parts:
            w.append(near(start, momenta, rows[h], rows[h], 0))
        w = list(lax.optimization_barrier(tuple(w)))
        column = jnp.concatenate(
            [jnp.sum(start, axis=0, keepdims=True), jnp.zeros((1, cells), jnp.float32)], axis=1
        )
        for turn in range(2):
            for h in parts:
                halo, carry = flight[h]
                before = column if turn == 1 else None
                scales = relay_call(coef, halo) if turn == 0 and h == 0 else coef
                far = functools.partial(far_call, meta, given, scales, blocks)
                v[h], x[h], halo, *after, carry = far(
                    x[h], w[h], halo, carry, chains, rows[h], turn, cap, before
                )
                if after:
                    (column,) = after
                flight[h] = (passed_along(halo, -1), passed_along(carry, 1))
                rows[h] = 0
                w[h] = near(x[h], v[h], 0, 0, 1 - turn)
                w = list(lax.optimization_barrier(tuple(w)))
        reach, columns = 1, [column]
        while reach < lax.axis_size("grp"):
            column = add_call(*columns) if reach > 1 else column
            pairs = [(g, g ^ reach) for g in range(lax.axis_size("grp"))]
            other = lax.ppermute(column, "grp", pairs)
            if reach == 1:
                other, w[1] = lax.optimization_barrier((other, w[1]))
            columns = [column, other]
            reach *= 2
        position, offset, gain = spread_call(start, x, columns, side, chain_total)
        momentum, dots = None, []
        for h in parts:
            momentum, dot = far(
                None, w[h], *flight[h], chains, 0, 0, cap, None, offset, momentum, h * chains
            )
            dots.append(dot)
        over = jnp.full((8, 8), (tiles[1] > cap).astype(jnp.float32))
        sums = summed_over("rows", jnp.concatenate([gain, *dots, over], axis=1))[0]
        spread, inner = sums[:local_chains], sums[local_chains : 2 * local_chains]
        chees = trajectory * (spread / all_cells) * (inner / all_cells)
        return sums[-1], position, momentum, chees

    cap = min(CAP, bands)
    results = two_steps(cap, start, momenta)
    if cap < bands:
        results = lax.while_loop(
            lambda state: state[0] > 0.0,
            lambda state: two_steps(
                bands,
                jnp.where(state[0] > 0.0, start, 0.0),
                jnp.where(state[0] > 0.0, momenta, 0.0),
            ),
            results,
        )
    return tuple(results[1:])


def solution(mesh):
    placed = (
        P("grp", "rows"),
        P("grp", "rows"),
        P("rows"),
        P("rows"),
        P("rows", None, None, None),
        P("rows", None),
        P("rows"),
        P(),
        P("grp"),
    )
    return jax.shard_map(
        on_device,
        mesh=mesh,
        in_specs=placed,
        out_specs=(P("grp", "rows"), P("grp", "rows"), P("grp")),
        check_vma=False,
    )
```

```python
import functools

import jax
import jax.numpy as jnp
from jax import lax
from jax.experimental import pallas as pl
from jax.experimental.pallas import tpu as pltpu
from jax.sharding import PartitionSpec as P

CHUNKS = 2
GROUP = 12
CAP = 45
VMEM_LIMIT = 60 * 2**20
LIST_AT = 8
ROW_AT = 128
SLOT_AT = 384
PLACE_AT = 640
META = 896

NT = (((1,), (1,)), ((), ()))
NN = (((1,), (0,)), ((), ()))


def passed_along(value, steps):
    count = lax.axis_size("rows")
    pairs = [(source, (source + steps) % count) for source in range(count)]
    return lax.ppermute(value, "rows", pairs)


def product(left, right, dims):
    return lax.dot_general(left, right, dims, preferred_element_type=jnp.float32)


def halves(value):
    high = value.astype(jnp.bfloat16)
    low = (value - high.astype(jnp.float32)).astype(jnp.bfloat16)
    return high, low


def doubled(own, chains):
    top = jnp.concatenate([own[:chains], jnp.zeros_like(own[:chains])], axis=0)
    return jnp.concatenate([own, top], axis=1)


def folded_up(value, chains, side):
    return value[:chains, :side] + (value[:chains, side:] + value[chains:, :side])


def stacked(block):
    high, low = halves(block)
    return jnp.concatenate([high, low], axis=0)


def local_column(cols_ref, r, s, first, bands, nblocks):
    raw = cols_ref[s, r] - first
    return jnp.where(raw < 0, raw + nblocks, raw)


def tiles_kernel(first_ref, cols_ref, count_ref, tiles_ref, place_ref, *, bands, slots, nblocks):
    first = first_ref[0]

    def clear(i, _):
        place_ref[i] = 0
        return 0

    lax.fori_loop(0, bands, clear, 0, unroll=8)

    def by_row(r, _):
        live = count_ref[r]
        for s in range(1, slots):
            col = local_column(cols_ref, r, s, first, bands, nblocks)
            far = jnp.logical_and(s < live, col >= bands)
            place_ref[jnp.where(far, col - bands, bands)] = 1
        return 0

    lax.fori_loop(0, bands, by_row, 0, unroll=4)

    def by_tile(m, tiles):
        tiles_ref[LIST_AT + tiles] = m
        used = place_ref[m]
        place_ref[m] = tiles
        return tiles + used

    tiles_ref[1] = lax.fori_loop(0, bands, by_tile, jnp.int32(0), unroll=4)


def edges_kernel(
    first_ref, cols_ref, count_ref, place_ref, far_ref, near_ref, *, bands, slots, nblocks
):
    first = first_ref[0]

    def by_row(r, counts):
        edges, nears = counts
        live = count_ref[r]
        for s in range(1, slots):
            col = local_column(cols_ref, r, s, first, bands, nblocks)
            is_live = s < live
            near = jnp.logical_and(is_live, col < bands)
            far = jnp.logical_and(is_live, col >= bands)
            far_ref[ROW_AT + edges] = r
            far_ref[SLOT_AT + edges] = s
            far_ref[PLACE_AT + edges] = place_ref[jnp.where(far, col - bands, 0)]
            near_ref[ROW_AT + nears] = r
            near_ref[SLOT_AT + nears] = s
            near_ref[PLACE_AT + nears] = col
            edges = edges + far.astype(jnp.int32)
            nears = nears + near.astype(jnp.int32)
        return edges, nears

    edges, nears = lax.fori_loop(0, bands, by_row, (jnp.int32(0), jnp.int32(0)), unroll=4)
    far_ref[0] = edges
    near_ref[0] = nears
    for i in range(GROUP):
        far_ref[ROW_AT + edges + i] = bands
        far_ref[SLOT_AT + edges + i] = 0
        far_ref[PLACE_AT + edges + i] = bands
        near_ref[ROW_AT + nears + i] = bands
        near_ref[SLOT_AT + nears + i] = 0
        near_ref[PLACE_AT + nears + i] = bands


def near_kernel(
    list_ref, coef_ref, x_hbm, v_hbm, seen_ref, weight_ref, blocks_hbm, out_hbm,
    x_buf, v_buf, diag, raw, split, total, sems, diag_sems, sem_of,
    *, bands, side, x_row, v_row, scale_at,
):
    chains = x_buf.shape[0]
    cells = bands * side
    edges = list_ref[0]
    groups = lax.div(edges + GROUP - 1, GROUP)
    pieces = diag_sems.shape[0]
    piece = bands // pieces

    def tile_at(index):
        return pl.ds(pl.multiple_of(index * side, side), side)

    get_x = pltpu.make_async_copy(x_hbm.at[pl.ds(x_row, chains)], x_buf, sems.at[0])
    get_v = pltpu.make_async_copy(v_hbm.at[pl.ds(v_row, chains)], v_buf, sems.at[1])
    put_w = pltpu.make_async_copy(v_buf, out_hbm, sems.at[2])

    def fetch_diag(p):
        rows = pl.ds(p * piece, piece)
        return pltpu.make_async_copy(blocks_hbm.at[rows, 0], diag.at[rows], diag_sems.at[p])

    def fetch(e):
        return pltpu.make_async_copy(
            blocks_hbm.at[list_ref[ROW_AT + e], list_ref[SLOT_AT + e]], raw.at[e], sem_of.at[e]
        )

    get_x.start()
    for p in range(pieces):
        fetch_diag(p).start()

    def start_fetch(e, _):
        fetch(e).start()
        return 0

    lax.fori_loop(0, edges, start_fetch, 0)
    get_v.start()
    get_x.wait()
    high, low = halves(x_buf[...])
    split[:chains, :cells] = high
    split[chains:, :cells] = low
    split[:, cells:] = jnp.zeros((2 * chains, side), jnp.bfloat16)
    total[:, cells:] = jnp.zeros((chains, side), jnp.float32)

    def diag_piece(p, _):
        fetch_diag(p).wait()
        for i in range(piece):
            r = p * piece + i
            up = product(split[:, tile_at(r)], stacked(diag[r]), NT)
            total[:, tile_at(r)] = folded_up(up, chains, side)
        return 0

    lax.fori_loop(0, pieces, diag_piece, 0)

    def group(g, _):
        base = g * GROUP
        for i in range(GROUP):

            @pl.when(base + i < edges)
            def _():
                fetch(base + i).wait()

        ups, downs, rows, cols = [], [], [], []
        for i in range(GROUP):
            rows.append(list_ref[ROW_AT + base + i])
            cols.append(list_ref[PLACE_AT + base + i])
            value = stacked(raw[base + i])
            ups.append(folded_up(product(split[:, tile_at(cols[i])], value, NT), chains, side))
            down = product(doubled(split[:, tile_at(rows[i])], chains), value, NN)
            downs.append(down[:chains] + down[chains:])
        for i in range(GROUP):
            total[:, tile_at(rows[i])] += ups[i]
            total[:, tile_at(cols[i])] += downs[i]
        return 0

    lax.fori_loop(0, groups, group, 0)
    get_v.wait()
    pull = total[:, :cells] + weight_ref[...] * (x_buf[...] - seen_ref[...])
    v_buf[...] = v_buf[...] - coef_ref[scale_at] * pull
    put_w.start()
    put_w.wait()


def far_kernel(
    *refs, bands, side, cap, x_row, scale_at, receives, sends, ends, dots=False,
    out_row=0, follows=False, step_at=2,
):
    refs = list(refs)

    def take(count):
        taken = refs[:count]
        del refs[:count]
        return taken

    (meta_ref, blocks_hbm) = take(2)
    if receives:
        coef_ref, w_hbm, halo_hbm = take(3)
        given_ref, carry_hbm = take(2)
    if sends:
        (x_hbm,) = take(1)
    if ends:
        (before_ref,) = take(1)
    if dots:
        (off_hbm,) = take(1)
    if follows:
        take(1)
    if receives:
        (v_out,) = take(1)
    if dots:
        (dot_out,) = take(1)
    if receives and sends:
        x_out, halo_out = take(2)
    if ends:
        (column_out,) = take(1)
    if sends:
        (carry_out,) = take(1)
    raw, both, sem_of, sems = take(4)
    if receives:
        vel, halo_buf, halo_split, carry_buf = take(4)
    if receives and sends:
        (packed_buf,) = take(1)
    if dots:
        off_buf, sums = take(2)
    if sends:
        x_buf, split, sum_carry = take(3)
    chains = (vel if receives else x_buf).shape[0]
    cells = bands * side
    edges = meta_ref[0]
    groups = lax.div(edges + GROUP - 1, GROUP)

    def tile_at(index):
        return pl.ds(pl.multiple_of(index * side, side), side)

    def fetch(e):
        return pltpu.make_async_copy(
            blocks_hbm.at[meta_ref[ROW_AT + e], meta_ref[SLOT_AT + e]], raw.at[e], sem_of.at[e]
        )

    def start_fetch(e, _):
        fetch(e).start()
        return 0

    def await_group(base):
        for i in range(GROUP):

            @pl.when(base + i < edges)
            def _():
                fetch(base + i).wait()

    if sends:
        get_x = pltpu.make_async_copy(x_hbm.at[pl.ds(x_row, chains)], x_buf, sems.at[0])
    if receives:
        get_halo = pltpu.make_async_copy(halo_hbm, halo_buf, sems.at[1])
        get_w = pltpu.make_async_copy(w_hbm, vel.at[:, pl.ds(0, cells)], sems.at[2])
        v_target = v_out if sends else v_out.at[pl.ds(out_row, chains)]
        put_v = pltpu.make_async_copy(vel.at[:, pl.ds(0, cells)], v_target, sems.at[3])
        get_halo.start()
        get_w.start()
    if sends and not receives:
        get_x.start()
    lax.fori_loop(0, edges, start_fetch, 0)
    if receives:
        get_carry = pltpu.make_async_copy(carry_hbm, carry_buf, sems.at[4])
        get_carry.start()
    if receives and sends:
        get_x.start()
    if dots:
        get_off = pltpu.make_async_copy(off_hbm, off_buf, sems.at[5])
        get_off.start()

    if receives:
        scale = coef_ref[scale_at]
        get_halo.wait()
        high, low = halves(halo_buf[...])
        halo_split[:cap, :chains] = high
        halo_split[:cap, chains:] = low
        halo_split[cap] = jnp.zeros((2 * chains, side), jnp.bfloat16)
        get_w.wait()
        vel[:, cells:] = jnp.zeros((chains, side), jnp.float32)

        def up_group(g, _):
            base = g * GROUP
            await_group(base)
            sums, rows = [], []
            for i in range(GROUP):
                rows.append(meta_ref[ROW_AT + base + i])
                value = stacked(raw[base + i])
                if sends:
                    both[base + i] = value
                place = jnp.minimum(meta_ref[PLACE_AT + base + i], cap)
                sums.append(folded_up(product(halo_split[place], value, NT), chains, side))
            for i in range(GROUP):
                vel[:, tile_at(rows[i])] -= scale * sums[i]
            return 0

        lax.fori_loop(0, groups, up_group, 0)
    if receives:
        given = jnp.minimum(given_ref[1], cap)
        get_carry.wait()

        def add_carry(k, _):
            vel[:, tile_at(given_ref[LIST_AT + k])] -= scale * carry_buf[k]
            return 0

        lax.fori_loop(0, given, add_carry, 0)
    if receives:
        put_v.start()
    if dots:
        get_off.wait()
        dot_out[...] = chain_sums(lambda part: vel[:, part] * off_buf[:, part], sums, cells)
    if sends:
        get_x.wait()
    if receives and sends:
        x_buf[...] += coef_ref[step_at] * vel[:, :cells]
        put_x = pltpu.make_async_copy(x_buf, x_out, sems.at[5])
        put_x.start()
        if ends:
            column_out[:, :cells] = before_ref[:, :cells]
            column_out[:, cells:] = before_ref[:, cells:] + jnp.sum(
                x_buf[...], axis=0, keepdims=True
            )

        def pack(k, _):
            packed_buf[k] = x_buf[:, tile_at(given_ref[LIST_AT + k])]
            return 0

        lax.fori_loop(0, given, pack, 0)
        put_halo = pltpu.make_async_copy(packed_buf, halo_out, sems.at[6])
        put_halo.start()
    if sends:
        high, low = halves(x_buf[...])
        split[:chains, :cells] = high
        split[chains:, :cells] = low
        split[:, cells:] = jnp.zeros((2 * chains, side), jnp.bfloat16)
        sum_carry[...] = jnp.zeros_like(sum_carry)

        def down_group(g, _):
            base = g * GROUP
            if not receives:
                await_group(base)
            sums, places = [], []
            for i in range(GROUP):
                row = meta_ref[ROW_AT + base + i]
                places.append(jnp.minimum(meta_ref[PLACE_AT + base + i], cap))
                value = both[base + i] if receives else stacked(raw[base + i])
                down = product(doubled(split[:, tile_at(row)], chains), value, NN)
                sums.append(down[:chains] + down[chains:])
            for i in range(GROUP):
                sum_carry[places[i]] += sums[i]
            return 0

        lax.fori_loop(0, groups, down_group, 0)
        put_carry = pltpu.make_async_copy(sum_carry.at[pl.ds(0, cap)], carry_out, sems.at[7])
        put_carry.start()
        put_carry.wait()
    if receives and sends:
        put_x.wait()
        put_halo.wait()
    if receives:
        put_v.wait()


def pack_kernel(given_ref, x_ref, out_ref, *, cap):
    side = out_ref.shape[2]

    def pack(k, _):
        tile = pl.ds(pl.multiple_of(given_ref[LIST_AT + k] * side, side), side)
        out_ref[k] = x_ref[:, tile]
        return 0

    lax.fori_loop(0, jnp.minimum(given_ref[1], cap), pack, 0)


def chain_sums(piece, sums, cells):
    wide = sums.shape[1]
    side = wide // 4
    sums[...] = jnp.zeros_like(sums)

    def add(i, _):
        sums[...] += piece(pl.ds(pl.multiple_of(i * wide, wide), wide))
        return 0

    lax.fori_loop(0, cells // wide, add, 0, unroll=2)
    lanes = sum(sums[:, i * side : (i + 1) * side] for i in range(4))
    return lax.dot_general(
        jnp.ones((8, side), jnp.float32), lanes, NT,
        precision=lax.Precision.HIGHEST, preferred_element_type=jnp.float32,
    )


def spread_kernel(
    start_ref, x0_ref, x1_ref, v_ref, *refs, chain_total
):
    *column_refs, position_ref, offset_ref, gain_ref, dot_ref, sums, means = refs
    chains = x0_ref.shape[0]
    cells = start_ref.shape[1]
    means[...] = sum(ref[...] for ref in column_refs) / chain_total
    upper = pl.ds(0, chains)
    lower = pl.ds(chains, chains)

    def ends(part):
        mean_start = means[:, part]
        mean_end = means[:, pl.ds(pl.multiple_of(cells + part.start, 128), part.size)]
        x0 = x0_ref[:, part]
        x1 = x1_ref[:, part]
        position_ref[upper, part] = x0
        position_ref[lower, part] = x1
        off_start = start_ref[:, part] - mean_start
        off1 = x1 - mean_end
        offset_ref[:, part] = off1
        off_end = jnp.concatenate([x0 - mean_end, off1], axis=0)
        return off_end * off_end - off_start * off_start

    gain_ref[...] = chain_sums(ends, sums, cells)

    def first_dot(part):
        mean_end = means[:, pl.ds(pl.multiple_of(cells + part.start, 128), part.size)]
        return (x0_ref[:, part] - mean_end) * v_ref[:, part]

    dot_ref[...] = chain_sums(first_dot, sums.at[upper], cells)


SMEM = pl.BlockSpec(memory_space=pltpu.SMEM)
VMEM = pl.BlockSpec(memory_space=pltpu.VMEM)
ANY = pl.BlockSpec(memory_space=pl.ANY)
PARAMS = pltpu.CompilerParams(vmem_limit_bytes=VMEM_LIMIT)
COST = pl.CostEstimate(flops=1000, bytes_accessed=1000, transcendentals=0)


def near_call(near_list, coef, x, v, seen, weight, blocks, chains, x_row, v_row, scale_at):
    bands, slots, side, _ = blocks.shape
    cells = bands * side
    most = bands * (slots - 1) + GROUP
    pieces = 8 if bands % 8 == 0 else 1
    return pl.pallas_call(
        functools.partial(
            near_kernel, bands=bands, side=side, x_row=x_row, v_row=v_row, scale_at=scale_at
        ),
        out_shape=jax.ShapeDtypeStruct((chains, cells), jnp.float32),
        in_specs=[SMEM, SMEM, ANY, ANY, VMEM, VMEM, ANY],
        out_specs=ANY,
        scratch_shapes=[
            pltpu.VMEM((chains, cells), jnp.float32),
            pltpu.VMEM((chains, cells), jnp.float32),
            pltpu.VMEM((bands, side, side), jnp.float32),
            pltpu.VMEM((most, side, side), jnp.float32),
            pltpu.VMEM((2 * chains, cells + side), jnp.bfloat16),
            pltpu.VMEM((chains, cells + side), jnp.float32),
            pltpu.SemaphoreType.DMA((3,)),
            pltpu.SemaphoreType.DMA((pieces,)),
            pltpu.SemaphoreType.DMA((most,)),
        ],
        compiler_params=PARAMS,
        cost_estimate=COST,
        name="near",
    )(near_list, coef, x, v, seen, weight, blocks)


def far_call(
    meta, given, coef, blocks, x, w, halo, carry, chains, x_row, scale_at, cap, before=None,
    offset=None, earlier=None, out_row=0,
):
    bands, slots, side, _ = blocks.shape
    cells = bands * side
    receives, sends = w is not None, x is not None
    ends, dots, follows = before is not None, offset is not None, earlier is not None
    most = bands * (slots - 1) + GROUP
    state = jax.ShapeDtypeStruct((chains, cells), jnp.float32)
    parcel = jax.ShapeDtypeStruct((cap, chains, side), jnp.float32)
    in_specs, args = [SMEM, ANY], [meta, blocks]
    out_shape, out_specs = [], []
    scratch = [
        pltpu.VMEM((most, side, side), jnp.float32),
        pltpu.VMEM((most, 2 * side, side), jnp.bfloat16),
        pltpu.SemaphoreType.DMA((most,)),
        pltpu.SemaphoreType.DMA((8,)),
    ]
    if receives:
        in_specs += [SMEM, ANY, ANY, SMEM, ANY]
        args += [coef, w, halo, given, carry]
        full = jax.ShapeDtypeStruct((CHUNKS * chains, cells), jnp.float32)
        out_shape += [state if sends else full]
        out_specs += [ANY]
        scratch += [
            pltpu.VMEM((chains, cells + side), jnp.float32),
            pltpu.VMEM((cap, chains, side), jnp.float32),
            pltpu.VMEM((cap + 1, 2 * chains, side), jnp.bfloat16),
            pltpu.VMEM((cap, chains, side), jnp.float32),
        ]
    if receives and sends:
        out_shape += [state, parcel]
        out_specs += [ANY, ANY]
        if ends:
            out_shape += [jax.ShapeDtypeStruct(before.shape, jnp.float32)]
            out_specs += [VMEM]
        scratch += [pltpu.VMEM((cap, chains, side), jnp.float32)]
    if dots:
        in_specs += [ANY]
        args += [offset]
        out_shape += [jax.ShapeDtypeStruct((8, chains), jnp.float32)]
        out_specs += [VMEM]
        scratch += [
            pltpu.VMEM((chains, cells), jnp.float32),
            pltpu.VMEM((chains, 4 * side), jnp.float32),
        ]
    if sends:
        in_specs += [ANY]
        args += [x]
        out_shape += [parcel]
        out_specs += [ANY]
        scratch += [
            pltpu.VMEM((chains, cells), jnp.float32),
            pltpu.VMEM((2 * chains, cells + side), jnp.bfloat16),
            pltpu.VMEM((cap + 1, chains, side), jnp.float32),
        ]
    if ends:
        in_specs += [VMEM]
        args += [before]
    aliases = {}
    if follows:
        aliases = {len(args): 0}
        in_specs += [ANY]
        args += [earlier]
    return pl.pallas_call(
        functools.partial(
            far_kernel, bands=bands, side=side, cap=cap, x_row=x_row, scale_at=scale_at,
            receives=receives, sends=sends, ends=ends, dots=dots, out_row=out_row,
            follows=follows,
        ),
        out_shape=out_shape,
        in_specs=in_specs,
        out_specs=out_specs,
        scratch_shapes=scratch,
        input_output_aliases=aliases,
        compiler_params=PARAMS,
        cost_estimate=COST,
        name="far",
    )(*args)


def relay_kernel(coef_ref, parcel_ref, out_ref):
    for i in range(3):
        out_ref[i] = coef_ref[i]


def relay_call(coef, parcel):
    return pl.pallas_call(
        relay_kernel,
        out_shape=jax.ShapeDtypeStruct(coef.shape, coef.dtype),
        in_specs=[SMEM, ANY],
        out_specs=SMEM,
        cost_estimate=COST,
        name="relay",
    )(coef, parcel)


def pack_call(given, x, chains, part, cap, side):
    return pl.pallas_call(
        functools.partial(pack_kernel, cap=cap),
        out_shape=jax.ShapeDtypeStruct((cap, chains, side), jnp.float32),
        grid=(1,),
        in_specs=[SMEM, pl.BlockSpec((chains, x.shape[1]), lambda i: (part, 0))],
        out_specs=pl.BlockSpec((cap, chains, side), lambda i: (0, 0, 0)),
        compiler_params=PARAMS,
        cost_estimate=COST,
        name="pack",
    )(given, x)


def spread_call(start, x, v, columns, side, chain_total):
    local_chains, cells = start.shape
    chains = x[0].shape[0]
    return pl.pallas_call(
        functools.partial(spread_kernel, chain_total=chain_total),
        out_shape=[
            jax.ShapeDtypeStruct(start.shape, jnp.float32),
            jax.ShapeDtypeStruct((chains, cells), jnp.float32),
            jax.ShapeDtypeStruct((8, local_chains), jnp.float32),
            jax.ShapeDtypeStruct((8, chains), jnp.float32),
        ],
        grid=(1,),
        in_specs=[VMEM, VMEM, VMEM, pl.BlockSpec((chains, cells), lambda i: (0, 0))]
        + [VMEM] * len(columns),
        out_specs=[VMEM] * 4,
        scratch_shapes=[
            pltpu.VMEM((local_chains, 4 * side), jnp.float32),
            pltpu.VMEM((1, 2 * cells), jnp.float32),
        ],
        compiler_params=PARAMS,
        cost_estimate=COST,
        name="spread",
    )(start, *x, v, *columns)


def shared_over(axis, value):
    count = lax.axis_size(axis)
    shared = [value]
    for k in range(1, count):
        pairs = [(source, (source + k) % count) for source in range(count)]
        shared.append(lax.ppermute(value, axis, pairs))
    return shared


def summed_over(axis, value):
    count = lax.axis_size(axis)
    reach = 1
    while reach < count:
        radix = 4 if count % (4 * reach) == 0 and (reach > 1 or count == 4) else 2
        own = value
        for k in range(1, radix):
            pairs = [(source, source ^ (k * reach)) for source in range(count)]
            value = value + lax.ppermute(own, axis, pairs)
        reach *= radix
    return value


def on_device(
    start, momenta, observed, precision_obs, blocks, block_cols, block_count, step_size, trajectory
):
    bands, slots, side, _ = blocks.shape
    cells = bands * side
    local_chains = start.shape[0]
    chains = local_chains // CHUNKS
    nblocks = bands * lax.axis_size("rows")
    all_cells = cells * lax.axis_size("rows")
    chain_total = local_chains * lax.axis_size("grp")
    first = (lax.axis_index("rows") * bands).astype(jnp.int32).reshape(1)
    plan = (first, block_cols.T, block_count)
    sizes = dict(bands=bands, slots=slots, nblocks=nblocks)
    tiles, places = pl.pallas_call(
        functools.partial(tiles_kernel, **sizes),
        out_shape=[
            jax.ShapeDtypeStruct((ROW_AT,), jnp.int32),
            jax.ShapeDtypeStruct((bands + 8,), jnp.int32),
        ],
        in_specs=[SMEM] * 3,
        out_specs=[SMEM] * 2,
        cost_estimate=COST,
        name="tiles",
    )(*plan)
    given = passed_along(tiles, 1)
    meta, near_list = pl.pallas_call(
        functools.partial(edges_kernel, **sizes),
        out_shape=[jax.ShapeDtypeStruct((META,), jnp.int32)] * 2,
        in_specs=[SMEM] * 4,
        out_specs=[SMEM] * 2,
        cost_estimate=COST,
        name="edges",
    )(*plan, places)
    step_len = step_size[0]
    coef = jnp.stack([step_len / 2, step_len, step_len])
    seen = observed.reshape(1, cells)
    weight = precision_obs.reshape(1, cells)
    parts = range(CHUNKS)
    first_rows = [h * chains for h in parts]

    def near(x, v, x_row, v_row, scale_at):
        return near_call(
            near_list, coef, x, v, seen, weight, blocks, chains, x_row, v_row, scale_at
        )

    def two_steps(cap, start, momenta):
        x, v, w, flight = [start] * CHUNKS, [momenta] * CHUNKS, [], []
        rows = list(first_rows)
        edges = meta
        for h in parts:
            halo = pack_call(given, start, chains, h, cap, side)
            edges, halo = lax.optimization_barrier((edges, halo))
            (carry,) = far_call(
                edges, given, coef, blocks, start, None, None, None, chains, rows[h], 0, cap
            )
            flight.append((passed_along(halo, -1), passed_along(carry, 1)))
        for h in parts:
            w.append(near(start, momenta, rows[h], rows[h], 0))
        w = list(lax.optimization_barrier(tuple(w)))
        column = jnp.concatenate(
            [jnp.sum(start, axis=0, keepdims=True), jnp.zeros((1, cells), jnp.float32)], axis=1
        )
        for turn in range(2):
            for h in parts:
                halo, carry = flight[h]
                before = column if turn == 1 else None
                scales = relay_call(coef, halo) if turn == 0 and h == 0 else coef
                far = functools.partial(far_call, meta, given, scales, blocks)
                v[h], x[h], halo, *after, carry = far(
                    x[h], w[h], halo, carry, chains, rows[h], turn, cap, before
                )
                if after:
                    (column,) = after
                flight[h] = (passed_along(halo, -1), passed_along(carry, 1))
                rows[h] = 0
                w[h] = near(x[h], v[h], 0, 0, 1 - turn)
                w = list(lax.optimization_barrier(tuple(w)))
        column, w[1] = lax.optimization_barrier((column, w[1]))
        (momentum,) = far(None, w[0], *flight[0], chains, 0, 0, cap)
        position, offset, gain, dot = spread_call(
            start, x, momentum, shared_over("grp", column), side, chain_total
        )
        momentum, last_dot = far(
            None, w[1], *flight[1], chains, 0, 0, cap, None, offset, momentum, chains
        )
        over = jnp.full((8, 8), (tiles[1] > cap).astype(jnp.float32))
        sums = summed_over("rows", jnp.concatenate([gain, dot, last_dot, over], axis=1))[0]
        spread, inner = sums[:local_chains], sums[local_chains : 2 * local_chains]
        chees = trajectory * (spread / all_cells) * (inner / all_cells)
        return sums[-1], position, momentum, chees

    cap = min(CAP, bands)
    results = two_steps(cap, start, momenta)
    if cap < bands:
        results = lax.while_loop(
            lambda state: state[0] > 0.0,
            lambda state: two_steps(
                bands,
                jnp.where(state[0] > 0.0, start, 0.0),
                jnp.where(state[0] > 0.0, momenta, 0.0),
            ),
            results,
        )
    return tuple(results[1:])


def solution(mesh):
    placed = (
        P("grp", "rows"),
        P("grp", "rows"),
        P("rows"),
        P("rows"),
        P("rows", None, None, None),
        P("rows", None),
        P("rows"),
        P(),
        P("grp"),
    )
    return jax.shard_map(
        on_device,
        mesh=mesh,
        in_specs=placed,
        out_specs=(P("grp", "rows"), P("grp", "rows"), P("grp")),
        check_vma=False,
    )
```
